32 devices in a mesh: chan: 4 (over y, x), win: 8 (over z, core).
Axes of the slice: x: 2, y: 2, z: 4, core: 2. Of those that a mesh axis runs over, the one named last changes fastest.
Arguments:
- raw: bfloat16 [32, 3200, 1024], P('win', None, 'chan'), may hold values from -6 to 6
- offsets: int32 [32], P('win'), may hold values from 0 to 128
- quality: int32 [32, 1024], P('win', 'chan'), may hold values 0 or 1
Outputs:
- stack: bfloat16 [384, 2, 1024, 1024], P('win', None, 'chan')
The draws below stay inside these ranges and needn't reach their ends.
All inputs are finite; a program needn't handle non-finite values. No bound on the sum of `quality` on one device may be relied on, other than what follows from the above.
Results may differ from the reference program's by a relative error of at most 0.0064.
Values may be sent and summed in bfloat16 or wider, within the bound.
No kernel may reach another device: no remote copies, remote signals or barrier semaphores. Data moves between devices by JAX's collectives and lax.ppermute only.
A program may use at most 256 MiB of HBM per device.

```python
import math
import jax
import jax.numpy as jnp
from jax import lax

C = 1024
F = 384
L = 3072
FIRST_BIN = 60
SHIFT = 128
WINDOWS = 32
SEG = 3200


def with_ends(drawn, rng, low, largest):
    spot = [jax.random.randint(jax.random.fold_in(rng, axis), (), 0, length) for axis, length in enumerate(drawn.shape)]
    main_axis = drawn.shape.index(max(drawn.shape))
    next_to = spot[:main_axis] + [(spot[main_axis] + 1) % drawn.shape[main_axis]] + spot[main_axis + 1:]
    return drawn.at[tuple(spot)].set(low).at[tuple(next_to)].set(largest)


def levels(key, dims, cuts, least, largest):
    loudness, own = 1.0, jax.random.fold_in(key, 6)
    for axis_at, shards_of in cuts:
        heights = jnp.exp(jax.random.uniform(jax.random.fold_in(own, axis_at), (shards_of,), jnp.float32, least / len(cuts), largest / len(cuts)))
        loudness = loudness * jnp.repeat(heights, dims[axis_at] // shards_of).reshape([-1 if axis == axis_at else 1 for axis in range(len(dims))])
    return loudness


def scatter_about(stream_key, shape, spread, limit, cuts=(), kind=jnp.bfloat16):
    loudness = levels(stream_key, shape, cuts, -0.22, 0.18) if cuts else 1.0
    values = jax.random.normal(stream_key, shape, jnp.float32) * spread * loudness
    return jnp.minimum(jnp.maximum(values, -limit), limit).astype(kind)


def setup_inputs(seed: int = 0) -> dict:
    arg_keys = jax.random.split(jax.random.key(seed), 4)
    raw = scatter_about(arg_keys[0], (WINDOWS, SEG, C), 1.0, 6.0, ((0, 8), (2, 4)))
    offsets = with_ends(jax.random.randint(arg_keys[1], (WINDOWS,), 0, SHIFT + 1), jax.random.fold_in(arg_keys[1], 1), 0, SHIFT).astype(jnp.int32)
    quality = with_ends((jax.random.randint(arg_keys[2], (WINDOWS, C), 0, 8) < 7).astype(jnp.int32), jax.random.fold_in(arg_keys[2], 1), 0, 1)
    return {"raw": raw, "offsets": offsets, "quality": quality}


epsilon = 1e-05

def dft_table():
    sample_idx = jnp.arange(L, dtype=jnp.int32)
    bin_idx = FIRST_BIN + jnp.arange(F, dtype=jnp.int32)
    residue = bin_idx[:, None] * sample_idx[None, :] % L
    angles = residue.astype(jnp.float32) * (2.0 * math.pi / L)
    return jnp.concatenate([jnp.cos(angles), -jnp.sin(angles)], 0).astype(jnp.bfloat16)

def reference(raw, offsets, quality):
    table = dft_table().astype(jnp.float32)

    def transform_window(record):
        segment, shift_at, usable = record
        samples = lax.dynamic_slice_in_dim(segment, shift_at.astype(jnp.int32), L, 0).astype(jnp.float32)
        transform = jnp.dot(table, samples, preferred_element_type=jnp.float32, precision=lax.Precision.HIGHEST)
        band_power = lax.optimization_barrier(jnp.sum(transform * transform, axis=0)) / F
        whiten = lax.rsqrt(band_power + epsilon) * usable.astype(jnp.float32)
        return (transform * whiten[None, :]).reshape(2, F, C).astype(jnp.bfloat16)
    spectra = lax.map(transform_window, (raw, offsets, quality))
    by_bin = jnp.moveaxis(spectra, 2, 0)
    stack_scale = 1.0 / math.sqrt(WINDOWS)

    def bin_stack(values):
        real_in = values[:, 0, :].astype(jnp.float32)
        imag_in = values[:, 1, :].astype(jnp.float32)
        high = lax.Precision.HIGHEST
        real_part = jnp.dot(real_in.T, real_in, precision=high) + jnp.dot(imag_in.T, imag_in, precision=high)
        imag_part = jnp.dot(imag_in.T, real_in, precision=high) - jnp.dot(real_in.T, imag_in, precision=high)
        return (jnp.stack([real_part, imag_part], 0) * stack_scale).astype(jnp.bfloat16)
    return lax.map(bin_stack, by_bin)
```

```python
import functools
import math

import jax
import jax.numpy as jnp
import ml_dtypes
import numpy as np
from jax import lax
from jax.experimental import pallas as pl
from jax.experimental.pallas import tpu as pltpu
from jax.sharding import PartitionSpec as P

F = 384
L = 3072
FIRST_BIN = 60
CHUNKS = 1

epsilon = 1e-05
VMEM_LIMIT = 56 * 1024 * 1024


def dft_table():
    sample_idx = np.arange(L, dtype=np.int64)
    bin_idx = FIRST_BIN + np.arange(F, dtype=np.int64)
    residue = bin_idx[:, None] * sample_idx[None, :] % L
    angles = residue.astype(np.float32) * np.float32(2.0 * math.pi / L)
    return np.concatenate([np.cos(angles), -np.sin(angles)], 0).astype(ml_dtypes.bfloat16)


def interleave(windows, bins):
    pair = 16 // (2 * windows)
    out = np.zeros((2 * windows * bins, 2 * windows * bins), np.float32)
    for f in range(bins):
        for p in range(2):
            for w in range(windows):
                row = ((f // pair * 2 + p) * pair + f % pair) * windows + w
                out[row, (w * 2 + p) * bins + f] = 1.0
    return out.astype(ml_dtypes.bfloat16)


def spectra_kernel(chunk_sizes, offsets_ref, table_ref, mix_ref, raw_ref, quality_ref, *refs):
    outs = refs[: len(chunk_sizes)]
    wide, window, white = refs[len(chunk_sizes) :]
    w = pl.program_id(0)
    windows = white.shape[0]
    seg, width = raw_ref.shape[1:]
    tile = 256

    wide[:seg] = raw_ref[0].astype(jnp.float32)
    shift_at = offsets_ref[w]
    coarse = shift_at // 8
    fine = shift_at - coarse * 8
    back = jnp.where(fine == 0, 0, 8 - fine)

    def cut(step, carry):
        start = pl.multiple_of((coarse + step * (tile // 8)) * 8, 8)
        rows = wide[pl.ds(start, tile + 8), :].reshape(tile // 8 + 1, 8, width)
        rolled = pltpu.roll(rows, back, 1)
        keep = lax.broadcasted_iota(jnp.int32, (tile // 8, 8, width), 1) < 8 - fine
        moved = jnp.where(keep, rolled[:-1], rolled[1:])
        window[pl.ds(pl.multiple_of(step * tile, tile), tile), :] = moved.reshape(tile, width).astype(jnp.bfloat16)
        return carry

    lax.fori_loop(0, L // tile, cut, 0)

    transform = jnp.dot(table_ref[...], window[...], preferred_element_type=jnp.float32)
    band_power = jnp.sum(transform * transform, axis=0, keepdims=True) / F
    whiten = lax.rsqrt(band_power + epsilon) * quality_ref[0].astype(jnp.float32)
    white[w] = (transform * whiten).astype(jnp.bfloat16)

    @pl.when(w == windows - 1)
    def _():
        pair = 16 // (2 * windows)
        bins = mix_ref.shape[0] // (2 * windows)
        share = sum(chunk_sizes)
        for block in range(F // bins):
            parts = [
                white[v, p * F + block * bins : p * F + (block + 1) * bins, :]
                for v in range(windows)
                for p in range(2)
            ]
            mixed = jnp.dot(mix_ref[...], jnp.concatenate(parts, 0), preferred_element_type=jnp.float32)
            mixed = mixed.astype(jnp.bfloat16)
            for g in range(bins // pair):
                group = block * (bins // pair) + g
                dest, at = group // share, group % share
                chunk = 0
                while at >= chunk_sizes[chunk]:
                    at -= chunk_sizes[chunk]
                    chunk += 1
                outs[chunk][dest, at] = mixed[g * 16 : (g + 1) * 16, :]


def spectra(raw, offsets, quality, dests, chunk_sizes):
    windows, seg, width = raw.shape
    bins = 256 // (2 * windows)
    table = jnp.asarray(dft_table())
    mix = jnp.asarray(interleave(windows, bins))
    grid_spec = pltpu.PrefetchScalarGridSpec(
        num_scalar_prefetch=1,
        grid=(windows,),
        in_specs=[
            pl.BlockSpec(table.shape, lambda w, _: (0, 0)),
            pl.BlockSpec(mix.shape, lambda w, _: (0, 0)),
            pl.BlockSpec((1, seg, width), lambda w, _: (w, 0, 0)),
            pl.BlockSpec((1, 1, width), lambda w, _: (w, 0, 0)),
        ],
        out_specs=[pl.BlockSpec((dests, size, 16, width), lambda w, _: (0, 0, 0, 0)) for size in chunk_sizes],
        scratch_shapes=[
            pltpu.VMEM((seg + 8, width), jnp.float32),
            pltpu.VMEM((L, width), jnp.bfloat16),
            pltpu.VMEM((windows, 2 * F, width), jnp.bfloat16),
        ],
    )
    return pl.pallas_call(
        functools.partial(spectra_kernel, chunk_sizes),
        grid_spec=grid_spec,
        out_shape=[jax.ShapeDtypeStruct((dests, size, 16, width), jnp.bfloat16) for size in chunk_sizes],
        compiler_params=pltpu.CompilerParams(vmem_limit_bytes=VMEM_LIMIT, dimension_semantics=("arbitrary",)),
        cost_estimate=pl.CostEstimate(
            flops=2 * windows * 2 * F * L * width, bytes_accessed=2 * windows * seg * width + 4 * F * L, transcendentals=0
        ),
        name="spectra",
    )(offsets, table, mix, raw, quality.reshape(windows, 1, width))


def stack_kernel(windows, scale, mine_ref, all_ref, *refs):
    out_ref = refs[-1]
    pair = 16 // (2 * windows)
    sources, _, rows, width = mine_ref.shape
    depth = sources * rows
    mine = mine_ref[:, 0].astype(jnp.float32)
    turned = jnp.concatenate([mine[:, 8:], -mine[:, :8]], 1)
    real_left = mine.reshape(depth, width).T.astype(jnp.bfloat16)
    imag_left = turned.reshape(depth, width).T.astype(jnp.bfloat16)
    bin_of = lax.broadcasted_iota(jnp.int32, (width, depth), 1) % 8 // windows
    lefts = []
    for b in range(pair):
        for left in (real_left, imag_left):
            lefts.append(jnp.where(bin_of == b, left, jnp.zeros_like(left)))
    for j in range(all_ref.shape[0]):
        right = all_ref[j, :, 0].reshape(depth, width)
        for n, left in enumerate(lefts):
            product = jnp.dot(left, right, preferred_element_type=jnp.float32)
            out_ref[n // 2, n % 2, :, j * width : (j + 1) * width] = (product * scale).astype(jnp.bfloat16)


def stack(mine, everyone, into, first_group, share, windows):
    sources, groups, rows, width = mine.shape
    blocks = everyone.shape[0]
    pair = 16 // (2 * windows)
    scale = 1.0 / math.sqrt(sources * windows)
    operands = [mine, everyone]
    in_specs = [
        pl.BlockSpec((sources, 1, rows, width), lambda g: (0, g, 0, 0)),
        pl.BlockSpec((blocks, sources, 1, rows, width), lambda g: (0, 0, g, 0, 0)),
    ]
    aliases = {}
    if into is not None:
        operands.append(into)
        in_specs.append(pl.BlockSpec(memory_space=pl.ANY))
        aliases = {2: 0}
    return pl.pallas_call(
        functools.partial(stack_kernel, windows, scale),
        grid=(groups,),
        in_specs=in_specs,
        out_specs=pl.BlockSpec((pair, 2, width, blocks * width), lambda g: (first_group + g, 0, 0, 0)),
        out_shape=jax.ShapeDtypeStruct((share * pair, 2, width, blocks * width), jnp.bfloat16),
        input_output_aliases=aliases,
        compiler_params=pltpu.CompilerParams(vmem_limit_bytes=VMEM_LIMIT, dimension_semantics=("arbitrary",)),
        cost_estimate=pl.CostEstimate(
            flops=8 * groups * pair * sources * rows * width * width * blocks,
            bytes_accessed=4 * groups * pair * width * blocks * width,
            transcendentals=0,
        ),
        name="stack",
    )(*operands)


def local(chunks, dests, raw, offsets, quality):
    windows = raw.shape[0]
    pair = 16 // (2 * windows)
    share = F // (dests * pair)
    while share % chunks:
        chunks -= 1
    chunk_sizes = [share // chunks] * chunks
    pieces = spectra(raw, offsets, quality, dests, chunk_sizes)
    out = None
    for chunk, piece in enumerate(pieces):
        mine = lax.all_to_all(piece, "win", split_axis=0, concat_axis=0, tiled=True)
        everyone = lax.all_gather(mine, "chan", axis=0, tiled=False)
        out = stack(mine, everyone, out, sum(chunk_sizes[:chunk]), share, windows)
    return out


def solution(mesh):
    in_specs = (P("win", None, "chan"), P("win"), P("win", "chan"))
    out_specs = P("win", None, "chan", None)
    run = functools.partial(local, CHUNKS, mesh.shape["win"])
    return jax.shard_map(run, mesh=mesh, in_specs=in_specs, out_specs=out_specs, check_vma=False)
```

```python
import functools
import math

import jax
import jax.numpy as jnp
import ml_dtypes
import numpy as np
from jax import lax
from jax.experimental import pallas as pl
from jax.experimental.pallas import tpu as pltpu
from jax.sharding import PartitionSpec as P

F = 384
L = 3072
FIRST_BIN = 60
CHUNKS = 4

epsilon = 1e-05
VMEM_LIMIT = 56 * 1024 * 1024


def dft_table():
    sample_idx = np.arange(L, dtype=np.int64)
    bin_idx = FIRST_BIN + np.arange(F, dtype=np.int64)
    residue = bin_idx[:, None] * sample_idx[None, :] % L
    angles = residue.astype(np.float32) * np.float32(2.0 * math.pi / L)
    return np.concatenate([np.cos(angles), -np.sin(angles)], 0).astype(ml_dtypes.bfloat16)


def interleave(windows, bins):
    pair = 16 // (2 * windows)
    out = np.zeros((2 * windows * bins, 2 * windows * bins), np.float32)
    for f in range(bins):
        for p in range(2):
            for w in range(windows):
                row = ((f // pair * 2 + p) * pair + f % pair) * windows + w
                out[row, (w * 2 + p) * bins + f] = 1.0
    return out.astype(ml_dtypes.bfloat16)


def spectra_kernel(chunk_sizes, offsets_ref, table_ref, mix_ref, raw_ref, quality_ref, *refs):
    outs = refs[: len(chunk_sizes)]
    wide, window, white = refs[len(chunk_sizes) :]
    w = pl.program_id(0)
    windows = white.shape[0]
    seg, width = raw_ref.shape[1:]
    tile = 256

    wide[:seg] = raw_ref[0].astype(jnp.float32)
    shift_at = offsets_ref[w]
    coarse = shift_at // 8
    fine = shift_at - coarse * 8
    back = jnp.where(fine == 0, 0, 8 - fine)

    def cut(step, carry):
        start = pl.multiple_of((coarse + step * (tile // 8)) * 8, 8)
        rows = wide[pl.ds(start, tile + 8), :].reshape(tile // 8 + 1, 8, width)
        rolled = pltpu.roll(rows, back, 1)
        keep = lax.broadcasted_iota(jnp.int32, (tile // 8, 8, width), 1) < 8 - fine
        moved = jnp.where(keep, rolled[:-1], rolled[1:])
        window[pl.ds(pl.multiple_of(step * tile, tile), tile), :] = moved.reshape(tile, width).astype(jnp.bfloat16)
        return carry

    lax.fori_loop(0, L // tile, cut, 0)

    transform = jnp.dot(table_ref[...], window[...], preferred_element_type=jnp.float32)
    band_power = jnp.sum(transform * transform, axis=0, keepdims=True) / F
    whiten = lax.rsqrt(band_power + epsilon) * quality_ref[0].astype(jnp.float32)
    white[w] = (transform * whiten).astype(jnp.bfloat16)

    @pl.when(w == windows - 1)
    def _():
        pair = 16 // (2 * windows)
        bins = mix_ref.shape[0] // (2 * windows)
        share = sum(chunk_sizes)
        for block in range(F // bins):
            parts = [
                white[v, p * F + block * bins : p * F + (block + 1) * bins, :]
                for v in range(windows)
                for p in range(2)
            ]
            mixed = jnp.dot(mix_ref[...], jnp.concatenate(parts, 0), preferred_element_type=jnp.float32)
            mixed = mixed.astype(jnp.bfloat16)
            for g in range(bins // pair):
                group = block * (bins // pair) + g
                dest, at = group // share, group % share
                chunk = 0
                while at >= chunk_sizes[chunk]:
                    at -= chunk_sizes[chunk]
                    chunk += 1
                outs[chunk][dest, at] = mixed[g * 16 : (g + 1) * 16, :]


def spectra(raw, offsets, quality, dests, chunk_sizes):
    windows, seg, width = raw.shape
    bins = 256 // (2 * windows)
    table = jnp.asarray(dft_table())
    mix = jnp.asarray(interleave(windows, bins))
    grid_spec = pltpu.PrefetchScalarGridSpec(
        num_scalar_prefetch=1,
        grid=(windows,),
        in_specs=[
            pl.BlockSpec(table.shape, lambda w, _: (0, 0)),
            pl.BlockSpec(mix.shape, lambda w, _: (0, 0)),
            pl.BlockSpec((1, seg, width), lambda w, _: (w, 0, 0)),
            pl.BlockSpec((1, 1, width), lambda w, _: (w, 0, 0)),
        ],
        out_specs=[pl.BlockSpec((dests, size, 16, width), lambda w, _: (0, 0, 0, 0)) for size in chunk_sizes],
        scratch_shapes=[
            pltpu.VMEM((seg + 8, width), jnp.float32),
            pltpu.VMEM((L, width), jnp.bfloat16),
            pltpu.VMEM((windows, 2 * F, width), jnp.bfloat16),
        ],
    )
    return pl.pallas_call(
        functools.partial(spectra_kernel, chunk_sizes),
        grid_spec=grid_spec,
        out_shape=[jax.ShapeDtypeStruct((dests, size, 16, width), jnp.bfloat16) for size in chunk_sizes],
        compiler_params=pltpu.CompilerParams(vmem_limit_bytes=VMEM_LIMIT, dimension_semantics=("arbitrary",)),
        cost_estimate=pl.CostEstimate(
            flops=2 * windows * 2 * F * L * width, bytes_accessed=2 * windows * seg * width + 4 * F * L, transcendentals=0
        ),
        name="spectra",
    )(offsets, table, mix, raw, quality.reshape(windows, 1, width))


def stack_kernel(windows, scale, mine_ref, all_ref, *refs):
    out_ref = refs[-1]
    pair = 16 // (2 * windows)
    sources, _, rows, width = mine_ref.shape
    depth = sources * rows
    mine = mine_ref[:, 0].astype(jnp.float32)
    turned = jnp.concatenate([mine[:, 8:], -mine[:, :8]], 1)
    real_left = mine.reshape(depth, width).T.astype(jnp.bfloat16)
    imag_left = turned.reshape(depth, width).T.astype(jnp.bfloat16)
    bin_of = lax.broadcasted_iota(jnp.int32, (width, depth), 1) % 8 // windows
    lefts = []
    for b in range(pair):
        for left in (real_left, imag_left):
            lefts.append(jnp.where(bin_of == b, left, jnp.zeros_like(left)))
    for j in range(all_ref.shape[0]):
        right = all_ref[j, :, 0].reshape(depth, width)
        for n, left in enumerate(lefts):
            product = jnp.dot(left, right, preferred_element_type=jnp.float32)
            out_ref[n // 2, n % 2, :, j * width : (j + 1) * width] = (product * scale).astype(jnp.bfloat16)


def stack(mine, everyone, into, first_group, share, windows):
    sources, groups, rows, width = mine.shape
    blocks = everyone.shape[0]
    pair = 16 // (2 * windows)
    scale = 1.0 / math.sqrt(sources * windows)
    operands = [mine, everyone]
    in_specs = [
        pl.BlockSpec((sources, 1, rows, width), lambda g: (0, g, 0, 0)),
        pl.BlockSpec((blocks, sources, 1, rows, width), lambda g: (0, 0, g, 0, 0)),
    ]
    aliases = {}
    if into is not None:
        operands.append(into)
        in_specs.append(pl.BlockSpec(memory_space=pl.ANY))
        aliases = {2: 0}
    return pl.pallas_call(
        functools.partial(stack_kernel, windows, scale),
        grid=(groups,),
        in_specs=in_specs,
        out_specs=pl.BlockSpec((pair, 2, width, blocks * width), lambda g: (first_group + g, 0, 0, 0)),
        out_shape=jax.ShapeDtypeStruct((share * pair, 2, width, blocks * width), jnp.bfloat16),
        input_output_aliases=aliases,
        compiler_params=pltpu.CompilerParams(vmem_limit_bytes=VMEM_LIMIT, dimension_semantics=("arbitrary",)),
        cost_estimate=pl.CostEstimate(
            flops=8 * groups * pair * sources * rows * width * width * blocks,
            bytes_accessed=4 * groups * pair * width * blocks * width,
            transcendentals=0,
        ),
        name="stack",
    )(*operands)


def local(chunks, dests, raw, offsets, quality):
    windows = raw.shape[0]
    pair = 16 // (2 * windows)
    share = F // (dests * pair)
    while share % chunks:
        chunks -= 1
    chunk_sizes = [share // chunks] * chunks
    pieces = spectra(raw, offsets, quality, dests, chunk_sizes)
    out = None
    for chunk, piece in enumerate(pieces):
        mine = lax.all_to_all(piece, "win", split_axis=0, concat_axis=0, tiled=True)
        everyone = lax.all_gather(mine, "chan", axis=0, tiled=False)
        out = stack(mine, everyone, out, sum(chunk_sizes[:chunk]), share, windows)
    return out


def solution(mesh):
    in_specs = (P("win", None, "chan"), P("win"), P("win", "chan"))
    out_specs = P("win", None, "chan", None)
    run = functools.partial(local, CHUNKS, mesh.shape["win"])
    return jax.shard_map(run, mesh=mesh, in_specs=in_specs, out_specs=out_specs, check_vma=False)
```

```python
import functools
import math

import jax
import jax.numpy as jnp
import ml_dtypes
import numpy as np
from jax import lax
from jax.experimental import pallas as pl
from jax.experimental.pallas import tpu as pltpu
from jax.sharding import PartitionSpec as P

F = 384
L = 3072
FIRST_BIN = 60
CHUNKS = 3

epsilon = 1e-05
VMEM_LIMIT = 56 * 1024 * 1024


def dft_table():
    sample_idx = np.arange(L, dtype=np.int64)
    bin_idx = FIRST_BIN + np.arange(F, dtype=np.int64)
    residue = bin_idx[:, None] * sample_idx[None, :] % L
    angles = residue.astype(np.float32) * np.float32(2.0 * math.pi / L)
    return np.concatenate([np.cos(angles), -np.sin(angles)], 0).astype(ml_dtypes.bfloat16)


def interleave(windows, bins):
    pair = 16 // (2 * windows)
    out = np.zeros((2 * windows * bins, 2 * windows * bins), np.float32)
    for f in range(bins):
        for p in range(2):
            for w in range(windows):
                row = ((f // pair * 2 + p) * pair + f % pair) * windows + w
                out[row, (w * 2 + p) * bins + f] = 1.0
    return out.astype(ml_dtypes.bfloat16)


def partner(one, other, members):
    if members & (members - 1) == 0:
        return one ^ other
    return (one + other) % members


def spectra_kernel(chunk_sizes, scalars_ref, table_ref, mix_ref, raw_ref, quality_ref, *refs):
    outs = refs[: len(chunk_sizes)]
    wide, window, white = refs[len(chunk_sizes) :]
    w = pl.program_id(0)
    windows = white.shape[0]
    seg, width = raw_ref.shape[1:]
    tile = 256

    wide[:seg] = raw_ref[0].astype(jnp.float32)
    shift_at = scalars_ref[w]
    coarse = shift_at // 8
    fine = shift_at - coarse * 8
    back = jnp.where(fine == 0, 0, 8 - fine)

    def cut(step, carry):
        start = pl.multiple_of((coarse + step * (tile // 8)) * 8, 8)
        rows = wide[pl.ds(start, tile + 8), :].reshape(tile // 8 + 1, 8, width)
        rolled = pltpu.roll(rows, back, 1)
        keep = lax.broadcasted_iota(jnp.int32, (tile // 8, 8, width), 1) < 8 - fine
        moved = jnp.where(keep, rolled[:-1], rolled[1:])
        window[pl.ds(pl.multiple_of(step * tile, tile), tile), :] = moved.reshape(tile, width).astype(jnp.bfloat16)
        return carry

    lax.fori_loop(0, L // tile, cut, 0)

    transform = jnp.dot(table_ref[...], window[...], preferred_element_type=jnp.float32)
    band_power = jnp.sum(transform * transform, axis=0, keepdims=True) / F
    whiten = lax.rsqrt(band_power + epsilon) * quality_ref[0].astype(jnp.float32)
    white[w] = (transform * whiten).astype(jnp.bfloat16)

    @pl.when(w == windows - 1)
    def _():
        pair = 16 // (2 * windows)
        bins = mix_ref.shape[0] // (2 * windows)
        share = sum(chunk_sizes)
        dests = outs[0].shape[0]
        for block in range(F // bins):
            parts = [
                white[v, p * F + block * bins : p * F + (block + 1) * bins, :]
                for v in range(windows)
                for p in range(2)
            ]
            mixed = jnp.dot(mix_ref[...], jnp.concatenate(parts, 0), preferred_element_type=jnp.float32)
            mixed = mixed.astype(jnp.bfloat16)
            for g in range(bins // pair):
                group = block * (bins // pair) + g
                dest, at = group // share, group % share
                chunk = 0
                while at >= chunk_sizes[chunk]:
                    at -= chunk_sizes[chunk]
                    chunk += 1
                outs[chunk][partner(dest, scalars_ref[windows], dests), at] = mixed[g * 16 : (g + 1) * 16, :]


def spectra(raw, offsets, quality, me, dests, chunk_sizes):
    windows, seg, width = raw.shape
    bins = 256 // (2 * windows)
    table = jnp.asarray(dft_table())
    mix = jnp.asarray(interleave(windows, bins))
    grid_spec = pltpu.PrefetchScalarGridSpec(
        num_scalar_prefetch=1,
        grid=(windows,),
        in_specs=[
            pl.BlockSpec(table.shape, lambda w, _: (0, 0)),
            pl.BlockSpec(mix.shape, lambda w, _: (0, 0)),
            pl.BlockSpec((1, seg, width), lambda w, _: (w, 0, 0)),
            pl.BlockSpec((1, 1, width), lambda w, _: (w, 0, 0)),
        ],
        out_specs=[pl.BlockSpec((dests, size, 16, width), lambda w, _: (0, 0, 0, 0)) for size in chunk_sizes],
        scratch_shapes=[
            pltpu.VMEM((seg + 8, width), jnp.float32),
            pltpu.VMEM((L, width), jnp.bfloat16),
            pltpu.VMEM((windows, 2 * F, width), jnp.bfloat16),
        ],
    )
    return pl.pallas_call(
        functools.partial(spectra_kernel, chunk_sizes),
        grid_spec=grid_spec,
        out_shape=[jax.ShapeDtypeStruct((dests, size, 16, width), jnp.bfloat16) for size in chunk_sizes],
        compiler_params=pltpu.CompilerParams(vmem_limit_bytes=VMEM_LIMIT, dimension_semantics=("arbitrary",)),
        cost_estimate=pl.CostEstimate(
            flops=2 * windows * 2 * F * L * width, bytes_accessed=2 * windows * seg * width + 4 * F * L, transcendentals=0
        ),
        name="spectra",
    )(jnp.append(offsets, me), table, mix, raw, quality.reshape(windows, 1, width))


def stack_kernel(windows, scale, half, place_ref, mine_ref, *refs):
    out_ref = refs[-1]
    pair = 16 // (2 * windows)
    sources, _, rows, width = mine_ref.shape
    depth = sources * rows
    mine = mine_ref[:, 0].astype(jnp.float32)
    turned = jnp.concatenate([mine[:, 8:], -mine[:, :8]], 1)
    real_left = mine.reshape(depth, width).T.astype(jnp.bfloat16)
    imag_left = turned.reshape(depth, width).T.astype(jnp.bfloat16)
    bin_of = lax.broadcasted_iota(jnp.int32, (width, depth), 1) % 8 // windows
    lefts = []
    for b in range(pair):
        for left in (real_left, imag_left):
            lefts.append(jnp.where(bin_of == b, left, jnp.zeros_like(left)))
    blocks = place_ref.shape[0]
    others = [[mine_ref]] + [[ref] for ref in refs[: blocks - 1 - half]]
    if half:
        others.append(list(refs[blocks - 2 : blocks]))
    for j, parts in enumerate(others):
        right = jnp.concatenate([part[:, 0].reshape(-1, width) for part in parts], 0)
        columns = pl.ds(pl.multiple_of(place_ref[j] * width, width), width)
        for n, left in enumerate(lefts):
            product = jnp.dot(left, right, preferred_element_type=jnp.float32)
            out_ref[n // 2, n % 2, :, columns] = (product * scale).astype(jnp.bfloat16)


def stack(place, mine, others, half, into, first_group, share, windows):
    sources, groups, rows, width = mine.shape
    blocks = place.shape[0]
    pair = 16 // (2 * windows)
    scale = 1.0 / math.sqrt(sources * windows)
    operands = [mine, *others]
    in_specs = [pl.BlockSpec((x.shape[0], 1, rows, width), lambda g, _: (0, g, 0, 0)) for x in operands]
    aliases = {}
    if into is not None:
        aliases = {1 + len(operands): 0}
        operands.append(into)
        in_specs.append(pl.BlockSpec(memory_space=pl.ANY))
    return pl.pallas_call(
        functools.partial(stack_kernel, windows, scale, half),
        grid_spec=pltpu.PrefetchScalarGridSpec(
            num_scalar_prefetch=1,
            grid=(groups,),
            in_specs=in_specs,
            out_specs=pl.BlockSpec((pair, 2, width, blocks * width), lambda g, _: (first_group + g, 0, 0, 0)),
        ),
        out_shape=jax.ShapeDtypeStruct((share * pair, 2, width, blocks * width), jnp.bfloat16),
        input_output_aliases=aliases,
        compiler_params=pltpu.CompilerParams(vmem_limit_bytes=VMEM_LIMIT, dimension_semantics=("arbitrary",)),
        cost_estimate=pl.CostEstimate(
            flops=8 * groups * pair * sources * rows * width * width * blocks,
            bytes_accessed=4 * groups * pair * width * blocks * width,
            transcendentals=0,
        ),
        name="stack",
    )(place, *operands)


def ring_order(members):
    half = members // 2
    return list(range(half)) + list(range(members - 1, half - 1, -1))


def ring_gather(x, members):
    ring = ring_order(members)
    ahead = [(ring[i], ring[(i + 1) % members]) for i in range(members)]
    back = [(ring[(i + 1) % members], ring[i]) for i in range(members)]
    left = right = x
    blocks, steps = [], []
    for step in range(1, (members + 1) // 2):
        left = lax.ppermute(left, "chan", ahead)
        right = lax.ppermute(right, "chan", back)
        blocks += [left, right]
        steps += [-step, step]
    half = members % 2 == 0
    if half:
        cut = x.shape[0] // 2
        blocks.append(lax.ppermute(left[:cut], "chan", ahead))
        blocks.append(lax.ppermute(right[cut:], "chan", back))
        steps.append(members // 2)
    ring = np.asarray(ring, np.int32)
    where = jnp.asarray(np.argsort(ring).astype(np.int32))[lax.axis_index("chan")]
    steps = np.asarray([0] + steps, np.int32)
    return jnp.asarray(ring)[(where + steps) % members], blocks, half


def swap(x, members):
    blocks = [x[0]]
    for k in range(1, members):
        pairs = [(i, partner(i, k, members)) for i in range(members)]
        if members & (members - 1):
            pairs = [(i, (k - i) % members) for i in range(members)]
        blocks.append(lax.ppermute(x[k], "win", pairs))
    return jnp.stack(blocks, 0)


def local(chunks, dests, members, raw, offsets, quality):
    windows = raw.shape[0]
    pair = 16 // (2 * windows)
    share = F // (dests * pair)
    while share % chunks:
        chunks -= 1
    chunk_sizes = [share // chunks] * chunks
    pieces = spectra(raw, offsets, quality, lax.axis_index("win"), dests, chunk_sizes)
    out = None
    for chunk, piece in enumerate(pieces):
        mine = swap(piece, dests)
        place, others, half = ring_gather(mine, members)
        out = stack(place, mine, others, half, out, sum(chunk_sizes[:chunk]), share, windows)
    return out


def solution(mesh):
    in_specs = (P("win", None, "chan"), P("win"), P("win", "chan"))
    out_specs = P("win", None, "chan", None)
    run = functools.partial(local, CHUNKS, mesh.shape["win"], mesh.shape["chan"])
    return jax.shard_map(run, mesh=mesh, in_specs=in_specs, out_specs=out_specs, check_vma=False)
```

```python
import functools
import math

import jax
import jax.numpy as jnp
import ml_dtypes
import numpy as np
from jax import lax
from jax.experimental import pallas as pl
from jax.experimental.pallas import tpu as pltpu
from jax.sharding import PartitionSpec as P

F = 384
L = 3072
FIRST_BIN = 60
CHUNK_WEIGHTS = (3, 3, 2)

epsilon = 1e-05
VMEM_LIMIT = 56 * 1024 * 1024


def dft_table():
    sample_idx = np.arange(L, dtype=np.int64)
    bin_idx = FIRST_BIN + np.arange(F, dtype=np.int64)
    residue = bin_idx[:, None] * sample_idx[None, :] % L
    angles = residue.astype(np.float32) * np.float32(2.0 * math.pi / L)
    return np.concatenate([np.cos(angles), -np.sin(angles)], 0).astype(ml_dtypes.bfloat16)


def interleave(windows, bins):
    pair = 16 // (2 * windows)
    out = np.zeros((2 * windows * bins, 2 * windows * bins), np.float32)
    for f in range(bins):
        for p in range(2):
            for w in range(windows):
                row = ((f // pair * 2 + p) * pair + f % pair) * windows + w
                out[row, (w * 2 + p) * bins + f] = 1.0
    return out.astype(ml_dtypes.bfloat16)


def partner(one, other, members):
    if members & (members - 1) == 0:
        return one ^ other
    return (one + other) % members


def spectra_kernel(offsets_ref, table_ref, mix_ref, raw_ref, quality_ref, keep_ref, give_ref, wide, window, white, mixed):
    w = pl.program_id(0)
    windows = white.shape[0]
    seg, width = raw_ref.shape[1:]
    tile = 256

    wide[:seg] = raw_ref[0].astype(jnp.float32)
    shift_at = offsets_ref[w]
    coarse = shift_at // 8
    fine = shift_at - coarse * 8
    back = jnp.where(fine == 0, 0, 8 - fine)

    def cut(step, carry):
        start = pl.multiple_of((coarse + step * (tile // 8)) * 8, 8)
        rows = wide[pl.ds(start, tile + 8), :].reshape(tile // 8 + 1, 8, width)
        rolled = pltpu.roll(rows, back, 1)
        keep = lax.broadcasted_iota(jnp.int32, (tile // 8, 8, width), 1) < 8 - fine
        moved = jnp.where(keep, rolled[:-1], rolled[1:])
        window[pl.ds(pl.multiple_of(step * tile, tile), tile), :] = moved.reshape(tile, width).astype(jnp.bfloat16)
        return carry

    lax.fori_loop(0, L // tile, cut, 0)

    transform = jnp.dot(table_ref[...], window[...], preferred_element_type=jnp.float32)
    band_power = jnp.sum(transform * transform, axis=0, keepdims=True) / F
    whiten = lax.rsqrt(band_power + epsilon) * quality_ref[pl.ds(w, 1), :].astype(jnp.float32)
    white[w] = (transform * whiten).astype(jnp.bfloat16)

    @pl.when(w == windows - 1)
    def _():
        pair = 16 // (2 * windows)
        bins = mix_ref.shape[0] // (2 * windows)
        groups = bins // pair
        for block in range(F // bins):
            parts = [
                white[v, p * F + block * bins : p * F + (block + 1) * bins, :]
                for v in range(windows)
                for p in range(2)
            ]
            product = jnp.dot(mix_ref[...], jnp.concatenate(parts, 0), preferred_element_type=jnp.float32)
            mixed[block * groups : (block + 1) * groups] = product.astype(jnp.bfloat16).reshape(groups, 16, width)
        me = lax.axis_index("win")
        chip, core = me // 2, me % 2
        chips, share = keep_ref.shape[:2]
        for k in range(chips):
            first = partner(chip, k, chips) * 2 * share
            keep_ref[k] = mixed[pl.ds(first + core * share, share)]
            give_ref[k] = mixed[pl.ds(first + (1 - core) * share, share)]


def spectra(raw, offsets, quality, dests):
    windows, seg, width = raw.shape
    bins = 256 // (2 * windows)
    groups = F * 2 * windows // 16
    table = jnp.asarray(dft_table())
    mix = jnp.asarray(interleave(windows, bins))
    blocks = (dests // 2, groups // dests, 16, width)
    grid_spec = pltpu.PrefetchScalarGridSpec(
        num_scalar_prefetch=1,
        grid=(windows,),
        in_specs=[
            pl.BlockSpec(table.shape, lambda w, _: (0, 0)),
            pl.BlockSpec(mix.shape, lambda w, _: (0, 0)),
            pl.BlockSpec((1, seg, width), lambda w, _: (w, 0, 0)),
            pl.BlockSpec((windows, width), lambda w, _: (0, 0)),
        ],
        out_specs=[pl.BlockSpec(blocks, lambda w, _: (0, 0, 0, 0))] * 2,
        scratch_shapes=[
            pltpu.VMEM((seg + 8, width), jnp.float32),
            pltpu.VMEM((L, width), jnp.bfloat16),
            pltpu.VMEM((windows, 2 * F, width), jnp.bfloat16),
            pltpu.VMEM((groups, 16, width), jnp.bfloat16),
        ],
    )
    return pl.pallas_call(
        spectra_kernel,
        grid_spec=grid_spec,
        out_shape=[jax.ShapeDtypeStruct(blocks, jnp.bfloat16)] * 2,
        compiler_params=pltpu.CompilerParams(vmem_limit_bytes=VMEM_LIMIT, dimension_semantics=("arbitrary",)),
        cost_estimate=pl.CostEstimate(
            flops=2 * windows * 2 * F * L * width, bytes_accessed=2 * windows * seg * width + 4 * F * L, transcendentals=0
        ),
        name="spectra",
    )(offsets, table, mix, raw, quality)


def join_kernel(moves, count, *refs):
    ins, outs, sems = refs[:count], refs[count:-1], refs[-1]
    copies = [
        pltpu.make_async_copy(ins[i].at[source], outs[o].at[dest], sems.at[n])
        for n, (i, source, o, dest) in enumerate(moves)
    ]
    for copy in copies:
        copy.start()
    for copy in copies:
        copy.wait()


def join(arrays, moves, out_shapes):
    return pl.pallas_call(
        functools.partial(join_kernel, moves, len(arrays)),
        in_specs=[pl.BlockSpec(memory_space=pl.ANY)] * len(arrays),
        out_specs=[pl.BlockSpec(memory_space=pl.ANY)] * len(out_shapes),
        out_shape=[jax.ShapeDtypeStruct(shape, arrays[0].dtype) for shape in out_shapes],
        scratch_shapes=[pltpu.SemaphoreType.DMA((len(moves),))],
        cost_estimate=pl.CostEstimate(
            flops=0, bytes_accessed=sum(4 * math.prod(shape) for shape in out_shapes), transcendentals=0
        ),
        name="join",
    )(*arrays)


def closed_walk(i, members):
    return jnp.where(i < members // 2, i, members - 1 - i + members // 2)


def stack_kernel(windows, scale, layout, *refs):
    out_ref = refs[-1]
    pair = 16 // (2 * windows)
    width = refs[0].shape[-1]

    def operand(indices):
        return jnp.concatenate([refs[i][:, 0].reshape(-1, width) for i in indices], 0)

    members = len(layout)
    where = closed_walk(lax.axis_index("chan"), members)
    mine = operand(layout[0][1])
    depth = mine.shape[0]
    mine = mine.astype(jnp.float32)
    by_part = mine.reshape(depth // 16, 16, width)
    turned = jnp.concatenate([by_part[:, 8:], -by_part[:, :8]], 1).reshape(depth, width)
    real_left = mine.T.astype(jnp.bfloat16)
    imag_left = turned.T.astype(jnp.bfloat16)
    bin_of = lax.broadcasted_iota(jnp.int32, (width, depth), 1) % 8 // windows
    lefts = []
    for b in range(pair):
        for left in (real_left, imag_left):
            lefts.append(jnp.where(bin_of == b, left, jnp.zeros_like(left)))
    for step, indices in layout:
        right = operand(indices)
        column = closed_walk(lax.rem(where + (step + members), members), members)
        columns = pl.ds(pl.multiple_of(column * width, width), width)
        for n, left in enumerate(lefts):
            product = jnp.dot(left, right, preferred_element_type=jnp.float32)
            out_ref[n // 2, n % 2, :, columns] = (product * scale).astype(jnp.bfloat16)


def stack(units, into, first_group, groups, share, windows, dests):
    members = len(units[0][0])
    rows, width = units[0][0][0][1][0].shape[2:]
    pair = 16 // (2 * windows)
    operands, in_specs, layout = [], [], []
    for n in range(members):
        indices = []
        for blocks, start in units:
            for x in blocks[n][1]:
                indices.append(len(operands))
                operands.append(x)
                at = first_group - start
                in_specs.append(pl.BlockSpec((x.shape[0], 1, rows, width), lambda g, at=at: (0, at + g, 0, 0)))
        layout.append((units[0][0][n][0], indices))
    aliases = {}
    if into is not None:
        aliases = {len(operands): 0}
        operands.append(into)
        in_specs.append(pl.BlockSpec(memory_space=pl.ANY))
    return pl.pallas_call(
        functools.partial(stack_kernel, windows, 1.0 / math.sqrt(dests * windows), layout),
        grid=(groups,),
        in_specs=in_specs,
        out_specs=pl.BlockSpec((pair, 2, width, members * width), lambda g: (first_group + g, 0, 0, 0)),
        out_shape=jax.ShapeDtypeStruct((share * pair, 2, width, members * width), jnp.bfloat16),
        input_output_aliases=aliases,
        compiler_params=pltpu.CompilerParams(vmem_limit_bytes=VMEM_LIMIT, dimension_semantics=("arbitrary",)),
        cost_estimate=pl.CostEstimate(
            flops=8 * groups * pair * dests * rows * width * width * members,
            bytes_accessed=4 * groups * pair * width * members * width,
            transcendentals=0,
        ),
        name="stack",
    )(*operands)


def after(arrays, *earlier):
    return lax.optimization_barrier((tuple(arrays), earlier))[0]


def ring_gather(x, members, before_last=None):
    ring = [i if i < members // 2 else members - 1 - i + members // 2 for i in range(members)]
    ahead = [(ring[i], ring[(i + 1) % members]) for i in range(members)]
    back = [(b, a) for a, b in ahead]
    left = right = x
    blocks = [(0, [x])]
    for step in range(1, (members + 1) // 2):
        left = lax.ppermute(left, "chan", ahead)
        right = lax.ppermute(right, "chan", back)
        blocks += [(-step, [left]), (step, [right])]
    if members % 2 == 0:
        cut = x.shape[0] // 2
        if before_last is not None:
            left, right = after((left, right), before_last)
        first = lax.ppermute(left[:cut], "chan", ahead)
        second = lax.ppermute(right[cut:], "chan", back)
        blocks.append((members // 2, [first, second]))
    return blocks


def chunk_starts(share):
    total, starts, seen = sum(CHUNK_WEIGHTS), [0], 0
    for weight in CHUNK_WEIGHTS:
        seen += weight
        starts.append(round(share * seen / total))
    return starts


def local(dests, members, raw, offsets, quality):
    windows, _, width = raw.shape
    pair = 16 // (2 * windows)
    share = F // (dests * pair)
    chips = dests // 2
    starts = chunk_starts(share)
    chunks = list(zip(starts[:-1], starts[1:]))

    keep, give = spectra(raw, offsets, quality, dests)
    other = lax.ppermute(give, "win", [(i, i ^ 1) for i in range(dests)])

    moves, shapes = [], [(2, share, 16, width)]
    for i in range(2):
        moves.append((i, 0, 0, i))
    for start, stop in chunks:
        for k in range(1, chips):
            for i in range(2):
                moves.append((i, (k, pl.ds(start, stop - start)), len(shapes), i))
            shapes.append((2, stop - start, 16, width))
    own, *far = join([keep, other], moves, shapes)

    def travel(x, k):
        pairs = []
        for i in range(dests):
            to = partner(i // 2, k, chips) if chips & (chips - 1) == 0 else (k - i // 2) % chips
            pairs.append((i, to * 2 + i % 2))
        return lax.ppermute(x, "win", pairs)

    own_blocks = ring_gather(own, members)
    earlier = [array for _, arrays in own_blocks[1:3] for array in arrays]
    first_pieces, arrived = [], []
    for n, (start, stop) in enumerate(chunks):
        sent = far[n * (chips - 1) : (n + 1) * (chips - 1)]
        if n > 0:
            sent = after(sent, *earlier)
            earlier = []
        pieces = [travel(x, k) for k, x in enumerate(sent, 1)]
        earlier = earlier + pieces[:1]
        first_pieces.append(pieces[0])
        shape = (2 * (chips - 1), stop - start, 16, width)
        moves = [(k, slice(None), 0, pl.ds(2 * k, 2)) for k in range(chips - 1)]
        arrived.append(join(pieces, moves, [shape])[0])
    out = None
    for n, (start, stop) in enumerate(chunks):
        blocks = ring_gather(arrived[n], members, out)
        if n + 2 < len(chunks):
            blocks[0] = (0, list(after(blocks[0][1], first_pieces[n + 2])))
        units = [(own_blocks, 0), (blocks, start)]
        out = stack(units, out, start, stop - start, share, windows, dests)
    return out


def solution(mesh):
    in_specs = (P("win", None, "chan"), P("win"), P("win", "chan"))
    out_specs = P("win", None, "chan", None)
    run = functools.partial(local, mesh.shape["win"], mesh.shape["chan"])
    return jax.shard_map(run, mesh=mesh, in_specs=in_specs, out_specs=out_specs, check_vma=False)
```

```python
import functools
import math

import jax
import jax.numpy as jnp
import ml_dtypes
import numpy as np
from jax import lax
from jax.experimental import pallas as pl
from jax.experimental.pallas import tpu as pltpu
from jax.sharding import PartitionSpec as P

F = 384
L = 3072
FIRST_BIN = 60
CHUNK_WEIGHTS = (3, 3, 2)

epsilon = 1e-05
MIB = 1024 * 1024


def dft_table():
    sample_idx = np.arange(L, dtype=np.int64)
    bin_idx = FIRST_BIN + np.arange(F, dtype=np.int64)
    residue = bin_idx[:, None] * sample_idx[None, :] % L
    angles = residue.astype(np.float32) * np.float32(2.0 * math.pi / L)
    return np.concatenate([np.cos(angles), -np.sin(angles)], 0).astype(ml_dtypes.bfloat16)


def interleave(windows, bins):
    pair = 16 // (2 * windows)
    out = np.zeros((2 * windows * bins, 2 * windows * bins), np.float32)
    for f in range(bins):
        for p in range(2):
            for w in range(windows):
                row = ((f // pair * 2 + p) * pair + f % pair) * windows + w
                out[row, (w * 2 + p) * bins + f] = 1.0
    return out.astype(ml_dtypes.bfloat16)


def partner(one, other, members):
    if members & (members - 1) == 0:
        return one ^ other
    return (one + other) % members


def spectra_kernel(offsets_ref, table_ref, mix_ref, raw_ref, quality_ref, keep_ref, give_ref, wide, window, white, mixed):
    w = pl.program_id(0)
    windows = white.shape[0]
    seg, width = raw_ref.shape[1:]
    tile = 256

    wide[:seg] = raw_ref[0].astype(jnp.float32)
    shift_at = offsets_ref[w]
    coarse = shift_at // 8
    fine = shift_at - coarse * 8
    back = jnp.where(fine == 0, 0, 8 - fine)

    def cut(step, carry):
        start = pl.multiple_of((coarse + step * (tile // 8)) * 8, 8)
        rows = wide[pl.ds(start, tile + 8), :].reshape(tile // 8 + 1, 8, width)
        rolled = pltpu.roll(rows, back, 1)
        keep = lax.broadcasted_iota(jnp.int32, (tile // 8, 8, width), 1) < 8 - fine
        moved = jnp.where(keep, rolled[:-1], rolled[1:])
        window[pl.ds(pl.multiple_of(step * tile, tile), tile), :] = moved.reshape(tile, width).astype(jnp.bfloat16)
        return carry

    lax.fori_loop(0, L // tile, cut, 0)

    transform = jnp.dot(table_ref[...], window[...], preferred_element_type=jnp.float32)
    band_power = jnp.sum(transform * transform, axis=0, keepdims=True) / F
    whiten = lax.rsqrt(band_power + epsilon) * quality_ref[pl.ds(w, 1), :].astype(jnp.float32)
    white[w] = (transform * whiten).astype(jnp.bfloat16)

    @pl.when(w == windows - 1)
    def _():
        pair = 16 // (2 * windows)
        bins = mix_ref.shape[0] // (2 * windows)
        groups = bins // pair
        for block in range(F // bins):
            parts = [
                white[v, p * F + block * bins : p * F + (block + 1) * bins, :]
                for v in range(windows)
                for p in range(2)
            ]
            product = jnp.dot(mix_ref[...], jnp.concatenate(parts, 0), preferred_element_type=jnp.float32)
            mixed[block * groups : (block + 1) * groups] = product.astype(jnp.bfloat16).reshape(groups, 16, width)
        me = lax.axis_index("win")
        chip, core = me // 2, me % 2
        chips, share = keep_ref.shape[:2]
        for k in range(chips):
            first = partner(chip, k, chips) * 2 * share
            keep_ref[k] = mixed[pl.ds(first + core * share, share)]
            give_ref[k] = mixed[pl.ds(first + (1 - core) * share, share)]


def spectra(raw, offsets, quality, dests):
    windows, seg, width = raw.shape
    bins = 256 // (2 * windows)
    groups = F * 2 * windows // 16
    table = jnp.asarray(dft_table())
    mix = jnp.asarray(interleave(windows, bins))
    blocks = (dests // 2, groups // dests, 16, width)
    grid_spec = pltpu.PrefetchScalarGridSpec(
        num_scalar_prefetch=1,
        grid=(windows,),
        in_specs=[
            pl.BlockSpec(table.shape, lambda w, _: (0, 0)),
            pl.BlockSpec(mix.shape, lambda w, _: (0, 0)),
            pl.BlockSpec((1, seg, width), lambda w, _: (w, 0, 0)),
            pl.BlockSpec((windows, width), lambda w, _: (0, 0)),
        ],
        out_specs=[pl.BlockSpec(blocks, lambda w, _: (0, 0, 0, 0))] * 2,
        scratch_shapes=[
            pltpu.VMEM((seg + 8, width), jnp.float32),
            pltpu.VMEM((L, width), jnp.bfloat16),
            pltpu.VMEM((windows, 2 * F, width), jnp.bfloat16),
            pltpu.VMEM((groups, 16, width), jnp.bfloat16),
        ],
    )
    return pl.pallas_call(
        spectra_kernel,
        grid_spec=grid_spec,
        out_shape=[jax.ShapeDtypeStruct(blocks, jnp.bfloat16)] * 2,
        compiler_params=pltpu.CompilerParams(vmem_limit_bytes=56 * MIB, dimension_semantics=("arbitrary",)),
        cost_estimate=pl.CostEstimate(
            flops=2 * windows * 2 * F * L * width, bytes_accessed=2 * windows * seg * width + 4 * F * L, transcendentals=0
        ),
        name="spectra",
    )(offsets, table, mix, raw, quality)


def join_kernel(moves, count, *refs):
    ins, outs = refs[:count], refs[count:]
    for i, source, o, dest in moves:
        outs[o][dest] = ins[i][source]


def join(arrays, moves, out_shapes):
    return pl.pallas_call(
        functools.partial(join_kernel, moves, len(arrays)),
        in_specs=[pl.BlockSpec(memory_space=pltpu.VMEM)] * len(arrays),
        out_specs=[pl.BlockSpec(memory_space=pltpu.VMEM)] * len(out_shapes),
        out_shape=[jax.ShapeDtypeStruct(shape, arrays[0].dtype) for shape in out_shapes],
        compiler_params=pltpu.CompilerParams(vmem_limit_bytes=16 * MIB),
        cost_estimate=pl.CostEstimate(
            flops=0, bytes_accessed=sum(4 * math.prod(shape) for shape in out_shapes), transcendentals=0
        ),
        name="join",
    )(*arrays)


def closed_walk(i, members):
    return jnp.where(i < members // 2, i, members - 1 - i + members // 2)


def stack_kernel(windows, scale, layout, *refs):
    out_ref = refs[-1]
    pair = 16 // (2 * windows)
    width = refs[0].shape[-1]

    def operand(indices):
        return jnp.concatenate([refs[i][:, 0].reshape(-1, width) for i in indices], 0)

    members = len(layout)
    where = closed_walk(lax.axis_index("chan"), members)
    mine = operand(layout[0][1])
    depth = mine.shape[0]
    mine = mine.astype(jnp.float32)
    by_part = mine.reshape(depth // 16, 16, width)
    turned = jnp.concatenate([by_part[:, 8:], -by_part[:, :8]], 1).reshape(depth, width)
    real_left = mine.T.astype(jnp.bfloat16)
    imag_left = turned.T.astype(jnp.bfloat16)
    bin_of = lax.broadcasted_iota(jnp.int32, (width, depth), 1) % 8 // windows
    lefts = []
    for b in range(pair):
        for left in (real_left, imag_left):
            lefts.append(jnp.where(bin_of == b, left, jnp.zeros_like(left)))
    for step, indices in layout:
        right = operand(indices)
        column = closed_walk(lax.rem(where + (step + members), members), members)
        columns = pl.ds(pl.multiple_of(column * width, width), width)
        for n, left in enumerate(lefts):
            product = jnp.dot(left, right, preferred_element_type=jnp.float32)
            out_ref[n // 2, n % 2, :, columns] = (product * scale).astype(jnp.bfloat16)


def stack(units, into, first_group, groups, share, windows, dests):
    members = len(units[0][0])
    rows, width = units[0][0][0][1][0].shape[2:]
    pair = 16 // (2 * windows)
    operands, in_specs, layout = [], [], []
    for n in range(members):
        indices = []
        for blocks, start in units:
            for x in blocks[n][1]:
                indices.append(len(operands))
                operands.append(x)
                at = first_group - start
                in_specs.append(pl.BlockSpec((x.shape[0], 1, rows, width), lambda g, at=at: (0, at + g, 0, 0)))
        layout.append((units[0][0][n][0], indices))
    aliases = {}
    if into is not None:
        aliases = {len(operands): 0}
        operands.append(into)
        in_specs.append(pl.BlockSpec(memory_space=pl.ANY))
    return pl.pallas_call(
        functools.partial(stack_kernel, windows, 1.0 / math.sqrt(dests * windows), layout),
        grid=(groups,),
        in_specs=in_specs,
        out_specs=pl.BlockSpec((pair, 2, width, members * width), lambda g: (first_group + g, 0, 0, 0)),
        out_shape=jax.ShapeDtypeStruct((share * pair, 2, width, members * width), jnp.bfloat16),
        input_output_aliases=aliases,
        compiler_params=pltpu.CompilerParams(vmem_limit_bytes=20 * MIB, dimension_semantics=("arbitrary",)),
        cost_estimate=pl.CostEstimate(
            flops=8 * groups * pair * dests * rows * width * width * members,
            bytes_accessed=4 * groups * pair * width * members * width,
            transcendentals=0,
        ),
        name="stack",
    )(*operands)


def after(arrays, *earlier):
    return lax.optimization_barrier((tuple(arrays), earlier))[0]


def ring_gather(x, members, before_last=None):
    ring = [i if i < members // 2 else members - 1 - i + members // 2 for i in range(members)]
    ahead = [(ring[i], ring[(i + 1) % members]) for i in range(members)]
    back = [(b, a) for a, b in ahead]
    left = right = x
    blocks = [(0, [x])]
    for step in range(1, (members + 1) // 2):
        left = lax.ppermute(left, "chan", ahead)
        right = lax.ppermute(right, "chan", back)
        blocks += [(-step, [left]), (step, [right])]
    if members % 2 == 0:
        cut = x.shape[0] // 2
        if before_last is not None:
            left, right = after((left, right), before_last)
        first = lax.ppermute(left[:cut], "chan", ahead)
        second = lax.ppermute(right[cut:], "chan", back)
        blocks.append((members // 2, [first, second]))
    return blocks


def chunk_starts(share):
    total, starts, seen = sum(CHUNK_WEIGHTS), [0], 0
    for weight in CHUNK_WEIGHTS:
        seen += weight
        starts.append(round(share * seen / total))
    return starts


def local(dests, members, raw, offsets, quality):
    windows, _, width = raw.shape
    pair = 16 // (2 * windows)
    share = F // (dests * pair)
    chips = dests // 2
    starts = chunk_starts(share)
    chunks = list(zip(starts[:-1], starts[1:]))

    keep, give = spectra(raw, offsets, quality, dests)
    other = lax.ppermute(give, "win", [(i, i ^ 1) for i in range(dests)])

    moves, shapes = [], [(2, share, 16, width)]
    for i in range(2):
        moves.append((i, 0, 0, i))
    for start, stop in chunks:
        for k in range(1, chips):
            for i in range(2):
                moves.append((i, (k, pl.ds(start, stop - start)), len(shapes), i))
            shapes.append((2, stop - start, 16, width))
    own, *far = join([keep, other], moves, shapes)

    def travel(x, k):
        pairs = []
        for i in range(dests):
            to = partner(i // 2, k, chips) if chips & (chips - 1) == 0 else (k - i // 2) % chips
            pairs.append((i, to * 2 + i % 2))
        return lax.ppermute(x, "win", pairs)

    own_blocks = ring_gather(own, members)
    earlier = [array for _, arrays in own_blocks[1:3] for array in arrays]
    first_pieces, arrived = [], []
    for n, (start, stop) in enumerate(chunks):
        sent = far[n * (chips - 1) : (n + 1) * (chips - 1)]
        if n > 0:
            sent = after(sent, *earlier)
            earlier = []
        pieces = [travel(x, k) for k, x in enumerate(sent, 1)]
        earlier = earlier + pieces[:1]
        first_pieces.append(pieces[0])
        shape = (2 * (chips - 1), stop - start, 16, width)
        moves = [(k, pl.ds(0, 2), 0, pl.ds(2 * k, 2)) for k in range(chips - 1)]
        arrived.append(join(pieces, moves, [shape])[0])
    out = None
    for n, (start, stop) in enumerate(chunks):
        blocks = ring_gather(arrived[n], members, out)
        if n + 2 < len(chunks):
            blocks[0] = (0, list(after(blocks[0][1], first_pieces[n + 2])))
        units = [(own_blocks, 0), (blocks, start)]
        out = stack(units, out, start, stop - start, share, windows, dests)
    return out


def solution(mesh):
    in_specs = (P("win", None, "chan"), P("win"), P("win", "chan"))
    out_specs = P("win", None, "chan", None)
    run = functools.partial(local, mesh.shape["win"], mesh.shape["chan"])
    return jax.shard_map(run, mesh=mesh, in_specs=in_specs, out_specs=out_specs, check_vma=False)
```

```python
import functools
import math

import jax
import jax.numpy as jnp
import ml_dtypes
import numpy as np
from jax import lax
from jax.experimental import pallas as pl
from jax.experimental.pallas import tpu as pltpu
from jax.sharding import PartitionSpec as P

F = 384
L = 3072
FIRST_BIN = 60
CHUNK_WEIGHTS = (3, 3, 2)

epsilon = 1e-05
MIB = 1024 * 1024


def dft_table():
    sample_idx = np.arange(L, dtype=np.int64)
    bin_idx = FIRST_BIN + np.arange(F, dtype=np.int64)
    residue = bin_idx[:, None] * sample_idx[None, :] % L
    angles = residue.astype(np.float32) * np.float32(2.0 * math.pi / L)
    return np.concatenate([np.cos(angles), -np.sin(angles)], 0).astype(ml_dtypes.bfloat16)


def interleave(windows, bins):
    pair = 16 // (2 * windows)
    out = np.zeros((2 * windows * bins, 2 * windows * bins), np.float32)
    for f in range(bins):
        for p in range(2):
            for w in range(windows):
                row = ((f // pair * 2 + p) * pair + f % pair) * windows + w
                out[row, (w * 2 + p) * bins + f] = 1.0
    return out.astype(ml_dtypes.bfloat16)


def partner(one, other, members):
    if members & (members - 1) == 0:
        return one ^ other
    return (one + other) % members


def spectra_kernel(offsets_ref, table_ref, mix_ref, raw_ref, quality_ref, keep_ref, give_ref, wide, window, white, mixed):
    w = pl.program_id(0)
    windows = white.shape[0]
    seg, width = raw_ref.shape[1:]
    tile = 256

    wide[:seg] = raw_ref[0].astype(jnp.float32)
    shift_at = offsets_ref[w]
    coarse = shift_at // 8
    fine = shift_at - coarse * 8
    back = jnp.where(fine == 0, 0, 8 - fine)

    def cut(step, carry):
        start = pl.multiple_of((coarse + step * (tile // 8)) * 8, 8)
        rows = wide[pl.ds(start, tile + 8), :].reshape(tile // 8 + 1, 8, width)
        rolled = pltpu.roll(rows, back, 1)
        keep = lax.broadcasted_iota(jnp.int32, (tile // 8, 8, width), 1) < 8 - fine
        moved = jnp.where(keep, rolled[:-1], rolled[1:])
        window[pl.ds(pl.multiple_of(step * tile, tile), tile), :] = moved.reshape(tile, width).astype(jnp.bfloat16)
        return carry

    lax.fori_loop(0, L // tile, cut, 0)

    transform = jnp.dot(table_ref[...], window[...], preferred_element_type=jnp.float32)
    band_power = jnp.sum(transform * transform, axis=0, keepdims=True) / F
    whiten = lax.rsqrt(band_power + epsilon) * quality_ref[pl.ds(w, 1), :].astype(jnp.float32)
    white[w] = (transform * whiten).astype(jnp.bfloat16)

    @pl.when(w == windows - 1)
    def _():
        pair = 16 // (2 * windows)
        bins = mix_ref.shape[0] // (2 * windows)
        groups = bins // pair
        for block in range(F // bins):
            parts = [
                white[v, p * F + block * bins : p * F + (block + 1) * bins, :]
                for v in range(windows)
                for p in range(2)
            ]
            product = jnp.dot(mix_ref[...], jnp.concatenate(parts, 0), preferred_element_type=jnp.float32)
            mixed[block * groups : (block + 1) * groups] = product.astype(jnp.bfloat16).reshape(groups, 16, width)
        me = lax.axis_index("win")
        chip, core = me // 2, me % 2
        chips, share = keep_ref.shape[:2]
        for k in range(chips):
            first = partner(chip, k, chips) * 2 * share
            keep_ref[k] = mixed[pl.ds(first + core * share, share)]
            give_ref[k] = mixed[pl.ds(first + (1 - core) * share, share)]


def spectra(raw, offsets, quality, dests):
    windows, seg, width = raw.shape
    bins = 256 // (2 * windows)
    groups = F * 2 * windows // 16
    table = jnp.asarray(dft_table())
    mix = jnp.asarray(interleave(windows, bins))
    blocks = (dests // 2, groups // dests, 16, width)
    grid_spec = pltpu.PrefetchScalarGridSpec(
        num_scalar_prefetch=1,
        grid=(windows,),
        in_specs=[
            pl.BlockSpec(table.shape, lambda w, _: (0, 0)),
            pl.BlockSpec(mix.shape, lambda w, _: (0, 0)),
            pl.BlockSpec((1, seg, width), lambda w, _: (w, 0, 0)),
            pl.BlockSpec((windows, width), lambda w, _: (0, 0)),
        ],
        out_specs=[pl.BlockSpec(blocks, lambda w, _: (0, 0, 0, 0))] * 2,
        scratch_shapes=[
            pltpu.VMEM((seg + 8, width), jnp.float32),
            pltpu.VMEM((L, width), jnp.bfloat16),
            pltpu.VMEM((windows, 2 * F, width), jnp.bfloat16),
            pltpu.VMEM((groups, 16, width), jnp.bfloat16),
        ],
    )
    return pl.pallas_call(
        spectra_kernel,
        grid_spec=grid_spec,
        out_shape=[jax.ShapeDtypeStruct(blocks, jnp.bfloat16)] * 2,
        compiler_params=pltpu.CompilerParams(vmem_limit_bytes=56 * MIB, dimension_semantics=("arbitrary",)),
        cost_estimate=pl.CostEstimate(
            flops=2 * windows * 2 * F * L * width, bytes_accessed=2 * windows * seg * width + 4 * F * L, transcendentals=0
        ),
        name="spectra",
    )(offsets, table, mix, raw, quality)


def join_kernel(moves, count, *refs):
    ins, outs = refs[:count], refs[count:]
    for i, source, o, dest in moves:
        outs[o][dest] = ins[i][source]


def join(arrays, moves, out_shapes):
    return pl.pallas_call(
        functools.partial(join_kernel, moves, len(arrays)),
        in_specs=[pl.BlockSpec(memory_space=pltpu.VMEM)] * len(arrays),
        out_specs=[pl.BlockSpec(memory_space=pltpu.VMEM)] * len(out_shapes),
        out_shape=[jax.ShapeDtypeStruct(shape, arrays[0].dtype) for shape in out_shapes],
        compiler_params=pltpu.CompilerParams(vmem_limit_bytes=16 * MIB),
        cost_estimate=pl.CostEstimate(
            flops=0, bytes_accessed=sum(4 * math.prod(shape) for shape in out_shapes), transcendentals=0
        ),
        name="join",
    )(*arrays)


def closed_walk(i, members):
    return jnp.where(i < members // 2, i, members - 1 - i + members // 2)


def stack_kernel(windows, scale, layout, *refs):
    out_ref = refs[-1]
    pair = 16 // (2 * windows)
    width = refs[0].shape[-1]

    def operand(indices):
        return jnp.concatenate([refs[i][:, 0].reshape(-1, width) for i in indices], 0)

    members = len(layout)
    where = closed_walk(lax.axis_index("chan"), members)
    mine = operand(layout[0][1])
    depth = mine.shape[0]
    by_part = mine.astype(jnp.float32).reshape(depth // 16, 16, width)
    turned = jnp.concatenate([by_part[:, 8:], -by_part[:, :8]], 1).reshape(depth, width).astype(jnp.bfloat16)
    row = lax.broadcasted_iota(jnp.int32, (width, width), 0)
    col = lax.broadcasted_iota(jnp.int32, (width, width), 1)
    eye = jnp.where(row == col, 1.0, 0.0).astype(jnp.bfloat16)
    bin_of = lax.broadcasted_iota(jnp.int32, (width, depth), 1) % 8 // windows
    flat = [
        lax.dot_general(eye, x, (((1,), (1,)), ((), ())), preferred_element_type=jnp.float32) for x in (mine, turned)
    ]
    lefts = [jnp.where(bin_of == b, x, 0.0).astype(jnp.bfloat16) for b in range(pair) for x in flat]
    left = jnp.concatenate(lefts, 0)
    for step, indices in layout:
        column = closed_walk(lax.rem(where + (step + members), members), members)
        columns = pl.ds(pl.multiple_of(column * width, width), width)
        product = jnp.dot(left, operand(indices), preferred_element_type=jnp.float32) * scale
        out_ref[:, :, :, columns] = product.astype(jnp.bfloat16).reshape(pair, 2, width, width)


def stack(units, into, first_group, groups, share, windows, dests):
    members = len(units[0][0])
    rows, width = units[0][0][0][1][0].shape[2:]
    pair = 16 // (2 * windows)
    operands, in_specs, layout = [], [], []
    for n in range(members):
        indices = []
        for blocks, start in units:
            for x in blocks[n][1]:
                indices.append(len(operands))
                operands.append(x)
                at = first_group - start
                in_specs.append(pl.BlockSpec((x.shape[0], 1, rows, width), lambda g, at=at: (0, at + g, 0, 0)))
        layout.append((units[0][0][n][0], indices))
    aliases = {}
    if into is not None:
        aliases = {len(operands): 0}
        operands.append(into)
        in_specs.append(pl.BlockSpec(memory_space=pl.ANY))
    return pl.pallas_call(
        functools.partial(stack_kernel, windows, 1.0 / math.sqrt(dests * windows), layout),
        grid=(groups,),
        in_specs=in_specs,
        out_specs=pl.BlockSpec((pair, 2, width, members * width), lambda g: (first_group + g, 0, 0, 0)),
        out_shape=jax.ShapeDtypeStruct((share * pair, 2, width, members * width), jnp.bfloat16),
        input_output_aliases=aliases,
        compiler_params=pltpu.CompilerParams(vmem_limit_bytes=20 * MIB, dimension_semantics=("arbitrary",)),
        cost_estimate=pl.CostEstimate(
            flops=8 * groups * pair * dests * rows * width * width * members,
            bytes_accessed=4 * groups * pair * width * members * width,
            transcendentals=0,
        ),
        name="stack",
    )(*operands)


def after(arrays, *earlier):
    return lax.optimization_barrier((tuple(arrays), earlier))[0]


def ring_gather(x, members, before_last=None):
    ring = [i if i < members // 2 else members - 1 - i + members // 2 for i in range(members)]
    ahead = [(ring[i], ring[(i + 1) % members]) for i in range(members)]
    back = [(b, a) for a, b in ahead]
    left = right = x
    blocks = [(0, [x])]
    for step in range(1, (members + 1) // 2):
        left = lax.ppermute(left, "chan", ahead)
        right = lax.ppermute(right, "chan", back)
        blocks += [(-step, [left]), (step, [right])]
    if members % 2 == 0:
        cut = x.shape[0] // 2
        if before_last is not None:
            left, right = after((left, right), before_last)
        first = lax.ppermute(left[:cut], "chan", ahead)
        second = lax.ppermute(right[cut:], "chan", back)
        blocks.append((members // 2, [first, second]))
    return blocks


def chunk_starts(share):
    total, starts, seen = sum(CHUNK_WEIGHTS), [0], 0
    for weight in CHUNK_WEIGHTS:
        seen += weight
        starts.append(round(share * seen / total))
    return starts


def local(dests, members, raw, offsets, quality):
    windows, _, width = raw.shape
    pair = 16 // (2 * windows)
    share = F // (dests * pair)
    chips = dests // 2
    starts = chunk_starts(share)
    chunks = list(zip(starts[:-1], starts[1:]))

    keep, give = spectra(raw, offsets, quality, dests)
    other = lax.ppermute(give, "win", [(i, i ^ 1) for i in range(dests)])

    moves, shapes = [], [(2, share, 16, width)]
    for i in range(2):
        moves.append((i, 0, 0, i))
    for start, stop in chunks:
        for k in range(1, chips):
            for i in range(2):
                moves.append((i, (k, pl.ds(start, stop - start)), len(shapes), i))
            shapes.append((2, stop - start, 16, width))
    own, *far = join([keep, other], moves, shapes)

    def travel(x, k):
        pairs = []
        for i in range(dests):
            to = partner(i // 2, k, chips) if chips & (chips - 1) == 0 else (k - i // 2) % chips
            pairs.append((i, to * 2 + i % 2))
        return lax.ppermute(x, "win", pairs)

    own_blocks = ring_gather(own, members)
    earlier = [array for _, arrays in own_blocks[1:3] for array in arrays]
    first_pieces, arrived = [], []
    for n, (start, stop) in enumerate(chunks):
        sent = far[n * (chips - 1) : (n + 1) * (chips - 1)]
        if n > 0:
            sent = after(sent, *earlier)
            earlier = []
        pieces = [travel(x, k) for k, x in enumerate(sent, 1)]
        earlier = earlier + pieces[:1]
        first_pieces.append(pieces[0])
        shape = (2 * (chips - 1), stop - start, 16, width)
        moves = [(k, pl.ds(0, 2), 0, pl.ds(2 * k, 2)) for k in range(chips - 1)]
        arrived.append(join(pieces, moves, [shape])[0])
    out = None
    for n, (start, stop) in enumerate(chunks):
        blocks = ring_gather(arrived[n], members, out)
        if n + 2 < len(chunks):
            blocks[0] = (0, list(after(blocks[0][1], first_pieces[n + 2])))
        units = [(own_blocks, 0), (blocks, start)]
        out = stack(units, out, start, stop - start, share, windows, dests)
    return out


def solution(mesh):
    in_specs = (P("win", None, "chan"), P("win"), P("win", "chan"))
    out_specs = P("win", None, "chan", None)
    run = functools.partial(local, mesh.shape["win"], mesh.shape["chan"])
    return jax.shard_map(run, mesh=mesh, in_specs=in_specs, out_specs=out_specs, check_vma=False)
```

```python
import functools
import math

import jax
import jax.numpy as jnp
import ml_dtypes
import numpy as np
from jax import lax
from jax.experimental import pallas as pl
from jax.experimental.pallas import tpu as pltpu
from jax.sharding import PartitionSpec as P

F = 384
L = 3072
FIRST_BIN = 60
CHUNK_WEIGHTS = (1, 1, 1)
STEP_GROUPS = 2

epsilon = 1e-05
MIB = 1024 * 1024


def dft_table():
    sample_idx = np.arange(L, dtype=np.int64)
    bin_idx = FIRST_BIN + np.arange(F, dtype=np.int64)
    residue = bin_idx[:, None] * sample_idx[None, :] % L
    angles = residue.astype(np.float32) * np.float32(2.0 * math.pi / L)
    return np.concatenate([np.cos(angles), -np.sin(angles)], 0).astype(ml_dtypes.bfloat16)


def interleave(windows, bins):
    pair = 16 // (2 * windows)
    out = np.zeros((2 * windows * bins, 2 * windows * bins), np.float32)
    for f in range(bins):
        for p in range(2):
            for w in range(windows):
                row = ((f // pair * 2 + p) * pair + f % pair) * windows + w
                out[row, (w * 2 + p) * bins + f] = 1.0
    return out.astype(ml_dtypes.bfloat16)


def cut(raw_ref, slot, shift_at, window_ref):
    width = raw_ref.shape[2]
    spare = raw_ref.shape[1] - L
    tile = 256
    base = jnp.minimum(shift_at // 16, (spare - 16) // 16) * 16
    rest = shift_at - base
    whole = rest // 8
    fine = rest - whole * 8
    back = jnp.where(fine == 0, 0, 8 - fine)
    keep = lax.broadcasted_iota(jnp.int32, (tile // 8, 8, width), 1) < 8 - fine
    count = tile // 8
    for step in range(L // tile):
        start = pl.multiple_of(base + step * tile, 16)
        rows = raw_ref[slot, pl.ds(start, tile + 16), :].astype(jnp.float32).reshape(count + 2, 8, width)
        rolled = pltpu.roll(rows, back, 1)
        upper = jnp.where(whole == 0, rolled[1 : count + 1], rolled[2:])
        lower = jnp.where(whole == 0, rolled[:count], jnp.where(whole == 1, rolled[1 : count + 1], rolled[2:]))
        moved = jnp.where(keep, lower, upper)
        window_ref[step * tile : (step + 1) * tile, :] = moved.reshape(tile, width).astype(jnp.bfloat16)


def spectra_kernel(offsets_ref, table_ref, mix_ref, raw_ref, quality_ref, keep_ref, give_ref, *scratch):
    white, mixed = scratch[:2]
    cuts = scratch[2:]
    windows, _, width = raw_ref.shape
    for w in range(windows):
        cut(raw_ref, w, offsets_ref[w], cuts[w])
        transform = jnp.dot(table_ref[...], cuts[w][...], preferred_element_type=jnp.float32)
        band_power = jnp.sum(transform * transform, axis=0, keepdims=True) / F
        usable = quality_ref[w : w + 1, :].astype(jnp.float32)
        white[w] = (transform * (lax.rsqrt(band_power + epsilon) * usable)).astype(jnp.bfloat16)

    pair = 16 // (2 * windows)
    bins = mix_ref.shape[0] // (2 * windows)
    groups = bins // pair
    for block in range(F // bins):
        parts = [
            white[v, p * F + block * bins : p * F + (block + 1) * bins, :] for v in range(windows) for p in range(2)
        ]
        product = jnp.dot(mix_ref[...], jnp.concatenate(parts, 0), preferred_element_type=jnp.float32)
        mixed[block * groups : (block + 1) * groups] = product.astype(jnp.bfloat16).reshape(groups, 16, width)
    me = lax.axis_index("win")
    chip, core = me // 2, me % 2
    chips, share = keep_ref.shape[:2]
    for k in range(chips):
        at = (chip ^ k) * 2 * share
        keep_ref[k] = mixed[pl.ds(at + core * share, share)]
        give_ref[k] = mixed[pl.ds(at + (1 - core) * share, share)]


def in_vmem(count):
    return [pl.BlockSpec(memory_space=pltpu.VMEM)] * count


def spectra(raw, offsets, quality, table, mix, dests):
    windows, _, width = raw.shape
    groups = F * 2 * windows // 16
    blocks = (dests // 2, groups // dests, 16, width)
    return pl.pallas_call(
        spectra_kernel,
        in_specs=[pl.BlockSpec(memory_space=pltpu.SMEM), *in_vmem(4)],
        out_specs=in_vmem(2),
        scratch_shapes=[
            pltpu.VMEM((windows, 2 * F, width), jnp.bfloat16),
            pltpu.VMEM((groups, 16, width), jnp.bfloat16),
            *[pltpu.VMEM((L, width), jnp.bfloat16)] * windows,
        ],
        out_shape=[jax.ShapeDtypeStruct(blocks, jnp.bfloat16)] * 2,
        compiler_params=pltpu.CompilerParams(vmem_limit_bytes=24 * MIB),
        cost_estimate=pl.CostEstimate(
            flops=2 * windows * 2 * F * L * width, bytes_accessed=2 * windows * raw.shape[1] * width + 4 * F * L, transcendentals=0
        ),
        name="spectra",
    )(offsets, table, mix, raw, quality)


def join_kernel(moves, *refs):
    out_ref = refs[-1]
    groups = out_ref.shape[1]
    to = 0
    for i, at, source, count in moves:
        out_ref[to : to + count] = refs[i][source : source + count, at : at + groups]
        to += count


def join(views, groups):
    arrays, moves = [], []
    for x, *where in views:
        known = [i for i, y in enumerate(arrays) if y is x]
        if not known:
            arrays.append(x)
        moves.append((known[0] if known else len(arrays) - 1, *where))
    shape = (sum(move[3] for move in moves), groups, *arrays[0].shape[2:])
    return pl.pallas_call(
        functools.partial(join_kernel, moves),
        in_specs=in_vmem(len(arrays)),
        out_specs=in_vmem(1)[0],
        out_shape=jax.ShapeDtypeStruct(shape, arrays[0].dtype),
        compiler_params=pltpu.CompilerParams(vmem_limit_bytes=12 * MIB),
        cost_estimate=pl.CostEstimate(flops=0, bytes_accessed=4 * math.prod(shape), transcendentals=0),
        name="join",
    )(*arrays)


def view(ref, group, at, sources):
    return ref[sources[0] : sources[1], group - at].reshape(-1, ref.shape[-1])


def turn_kernel(first_group, views, *refs):
    out_ref = refs[-1]
    _, _, width, depth = out_ref.shape

    def body(g, carry):
        x = jnp.concatenate([view(refs[i], first_group + g, *where) for i, where in enumerate(views)], 0)
        by_part = x.astype(jnp.float32).reshape(depth // 16, 16, width)
        turned = jnp.concatenate([by_part[:, 8:], -by_part[:, :8]], 1)
        out_ref[g, 0] = by_part.reshape(depth, width).T.astype(jnp.bfloat16)
        out_ref[g, 1] = turned.reshape(depth, width).T.astype(jnp.bfloat16)
        return carry

    lax.fori_loop(0, out_ref.shape[0], body, 0)


def turn(items, first_group, groups):
    rows, width = items[0][0].shape[2:]
    depth = sum(sources[1] - sources[0] for _, _, sources in items) * rows
    return pl.pallas_call(
        functools.partial(turn_kernel, first_group, [item[1:] for item in items]),
        in_specs=in_vmem(len(items)),
        out_specs=in_vmem(1)[0],
        out_shape=jax.ShapeDtypeStruct((groups, 2, width, depth), jnp.bfloat16),
        compiler_params=pltpu.CompilerParams(vmem_limit_bytes=12 * MIB),
        cost_estimate=pl.CostEstimate(flops=0, bytes_accessed=8 * groups * width * depth, transcendentals=0),
        name="turn",
    )(*[item[0] for item in items])


def closed_walk(i, members):
    return jnp.where(i < members // 2, i, members - 1 - i + members // 2)


def stack_kernel(windows, scale, first_group, layout, left_ref, *refs):
    out_ref = refs[-1]
    pair = 16 // (2 * windows)
    width, depth = left_ref.shape[2:]
    step_groups = out_ref.shape[0] // pair
    members = len(layout)
    where = closed_walk(lax.axis_index("chan"), members)
    bin_of = lax.broadcasted_iota(jnp.int32, (width, depth), 1) % 8 // windows
    masks = [jnp.where(bin_of == b, 1.0, 0.0).astype(jnp.bfloat16) for b in range(pair)]
    for s in range(step_groups):
        g = pl.program_id(0) * step_groups + s
        sides = [left_ref[g, part] for part in range(2)]
        for step, items in layout:
            right = jnp.concatenate([view(refs[i], first_group + g, *item) for i, item in items], 0)
            column = closed_walk(lax.rem(where + (step + members), members), members)
            columns = pl.ds(pl.multiple_of(column * width, width), width)
            for b in range(pair):
                for part in range(2):
                    product = jnp.dot(sides[part] * masks[b], right, preferred_element_type=jnp.float32)
                    out_ref[s * pair + b, part, :, columns] = (product * scale).astype(jnp.bfloat16)


def stack(left, steps, into, first_group, bins, windows, sources):
    members = len(steps)
    groups, _, width, depth = left.shape
    pair = 16 // (2 * windows)
    step_groups = max(n for n in range(1, STEP_GROUPS + 1) if groups % n == 0 and first_group % n == 0)
    operands, layout = [left], []
    for step, items in steps:
        layout.append((step, [(len(operands) - 1 + i, item[1:]) for i, item in enumerate(items)]))
        operands += [item[0] for item in items]
    in_specs = in_vmem(len(operands))
    aliases = {}
    if into is not None:
        aliases = {len(operands): 0}
        operands.append(into)
        in_specs.append(pl.BlockSpec(memory_space=pl.ANY))
    block = (step_groups * pair, 2, width, members * width)
    return pl.pallas_call(
        functools.partial(stack_kernel, windows, 1.0 / math.sqrt(sources), first_group, layout),
        grid=(groups // step_groups,),
        in_specs=in_specs,
        out_specs=pl.BlockSpec(block, lambda g: (first_group // step_groups + g, 0, 0, 0)),
        out_shape=jax.ShapeDtypeStruct((bins, 2, width, members * width), jnp.bfloat16),
        input_output_aliases=aliases,
        compiler_params=pltpu.CompilerParams(vmem_limit_bytes=24 * MIB, dimension_semantics=("arbitrary",)),
        cost_estimate=pl.CostEstimate(
            flops=4 * groups * pair * depth * width * width * members,
            bytes_accessed=4 * groups * pair * width * members * width,
            transcendentals=0,
        ),
        name="stack",
    )(*operands)


def after(arrays, *earlier):
    return list(lax.optimization_barrier((tuple(arrays), earlier))[0])


def ring_gather(x, members, before_last=None):
    ring = [i if i < members // 2 else members - 1 - i + members // 2 for i in range(members)]
    ahead = [(ring[i], ring[(i + 1) % members]) for i in range(members)]
    back = [(b, a) for a, b in ahead]
    left = right = x
    blocks = [(0, [x])]
    for step in range(1, (members + 1) // 2):
        left = lax.ppermute(left, "chan", ahead)
        right = lax.ppermute(right, "chan", back)
        blocks += [(-step, [left]), (step, [right])]
    if members % 2 == 0:
        cut_at = x.shape[0] // 2
        if before_last is not None:
            left, right = after((left, right), before_last)
        first = lax.ppermute(left[:cut_at], "chan", ahead)
        second = lax.ppermute(right[cut_at:], "chan", back)
        blocks.append((members // 2, [first, second]))
    return blocks


def neighbours(blocks):
    return [array for _, arrays in blocks[1:3] for array in arrays]


def chunk_starts(share):
    total, starts, seen = sum(CHUNK_WEIGHTS), [0], 0
    for weight in CHUNK_WEIGHTS:
        seen += weight
        starts.append(round(share * seen / total))
    return starts


def local(dests, members, raw, offsets, quality):
    windows = raw.shape[0]
    pair = 16 // (2 * windows)
    bins = F // dests
    share = bins // pair
    chips = dests // 2
    assert chips & (chips - 1) == 0
    starts = chunk_starts(share)
    chunks = list(zip(starts[:-1], starts[1:]))
    table = jnp.asarray(dft_table())
    mix = jnp.asarray(interleave(windows, 256 // (2 * windows)))

    keep, give = spectra(raw, offsets, quality, table, mix, dests)
    other = lax.ppermute(give, "win", [(i, i ^ 1) for i in range(dests)])
    own = join([(keep, 0, 0, 1), (other, 0, 0, 1)], share)
    own_blocks = ring_gather(own, members)

    arrived, first = [], None
    for start, stop in chunks:
        held = [[(keep, start, k, 1), (other, start, k, 1)] for k in range(chips)]
        across, sources = chips // 2, 2
        while across:
            sent = join(sum(held[across : 2 * across], []), stop - start)
            if first is not None and across == chips // 2:
                sent = after([sent], first)[0]
            elif first is not None and start == 0:
                sent = after([sent], *neighbours(own_blocks))[0]
            came = lax.ppermute(sent, "win", [(i, i ^ (2 * across)) for i in range(dests)])
            if across == chips // 2:
                first = came
            for k in range(across):
                held[k].append((came, 0, k * sources, sources))
            across, sources = across // 2, 2 * sources
        arrived.append(join(held[0][2:], stop - start))

    out = None
    for (start, stop), far in zip(chunks, arrived):
        blocks = ring_gather(far, members, out)
        steps = []
        for (step, own_arrays), (_, arrays) in zip(own_blocks, blocks):
            views = [(x, 0, (0, x.shape[0])) for x in own_arrays] + [(x, start, (0, x.shape[0])) for x in arrays]
            steps.append((step, views))
        left = turn(steps[0][1], start, stop - start)
        out = stack(left, steps, out, start, bins, windows, dests * windows)
    return out


def solution(mesh):
    in_specs = (P("win", None, "chan"), P("win"), P("win", "chan"))
    out_specs = P("win", None, "chan", None)
    run = functools.partial(local, mesh.shape["win"], mesh.shape["chan"])
    return jax.shard_map(run, mesh=mesh, in_specs=in_specs, out_specs=out_specs, check_vma=False)
```

```python
import functools
import math

import jax
import jax.numpy as jnp
import ml_dtypes
import numpy as np
from jax import lax
from jax.experimental import pallas as pl
from jax.experimental.pallas import tpu as pltpu
from jax.sharding import PartitionSpec as P

F = 384
L = 3072
FIRST_BIN = 60
UNITS = 2
STEP_GROUPS = 2
SPECTRA_MIB = 50

epsilon = 1e-05
MIB = 1024 * 1024


def dft_table():
    sample_idx = np.arange(L, dtype=np.int64)
    bin_idx = FIRST_BIN + np.arange(F, dtype=np.int64)
    residue = bin_idx[:, None] * sample_idx[None, :] % L
    angles = residue.astype(np.float32) * np.float32(2.0 * math.pi / L)
    return np.concatenate([np.cos(angles), -np.sin(angles)], 0).astype(ml_dtypes.bfloat16)


def interleave(windows, bins):
    pair = 16 // (2 * windows)
    out = np.zeros((2 * windows * bins, 2 * windows * bins), np.float32)
    for f in range(bins):
        for p in range(2):
            for w in range(windows):
                row = ((f // pair * 2 + p) * pair + f % pair) * windows + w
                out[row, (w * 2 + p) * bins + f] = 1.0
    return out.astype(ml_dtypes.bfloat16)


def cut(raw_ref, slot, shift_at, window_ref):
    width = raw_ref.shape[2]
    spare = raw_ref.shape[1] - L
    tile = 256
    base = jnp.minimum(shift_at // 16, (spare - 16) // 16) * 16
    rest = shift_at - base
    whole = rest // 8
    fine = rest - whole * 8
    back = jnp.where(fine == 0, 0, 8 - fine)
    keep = lax.broadcasted_iota(jnp.int32, (tile // 8, 8, width), 1) < 8 - fine
    count = tile // 8
    for step in range(L // tile):
        start = pl.multiple_of(base + step * tile, 16)
        rows = raw_ref[slot, pl.ds(start, tile + 16), :].astype(jnp.float32).reshape(count + 2, 8, width)
        rolled = pltpu.roll(rows, back, 1)
        upper = jnp.where(whole == 0, rolled[1 : count + 1], rolled[2:])
        lower = jnp.where(whole == 0, rolled[:count], jnp.where(whole == 1, rolled[1 : count + 1], rolled[2:]))
        moved = jnp.where(keep, lower, upper)
        window_ref[step * tile : (step + 1) * tile, :] = moved.reshape(tile, width).astype(jnp.bfloat16)


def spectra_kernel(offsets_ref, table_hbm, mix_hbm, raw_hbm, quality_hbm, keep_ref, give_ref, *scratch):
    table_ref, mix_ref, quality_ref, raw_ref, white, mixed, sems = scratch[:7]
    cuts = scratch[7:]
    windows, _, width = raw_ref.shape
    loads = [pltpu.make_async_copy(raw_hbm.at[w], raw_ref.at[w], sems.at[w]) for w in range(windows)]
    table_load = pltpu.make_async_copy(table_hbm, table_ref, sems.at[windows])
    mix_load = pltpu.make_async_copy(mix_hbm, mix_ref, sems.at[windows + 1])
    quality_load = pltpu.make_async_copy(quality_hbm, quality_ref, sems.at[windows + 2])
    for load in (loads[0], table_load, *loads[1:], quality_load, mix_load):
        load.start()
    for w in range(windows):
        loads[w].wait()
        cut(raw_ref, w, offsets_ref[w], cuts[w])
        if w == 0:
            table_load.wait()
        transform = jnp.dot(table_ref[...], cuts[w][...], preferred_element_type=jnp.float32)
        band_power = jnp.sum(transform * transform, axis=0, keepdims=True) / F
        if w == 0:
            quality_load.wait()
        usable = quality_ref[w : w + 1, :].astype(jnp.float32)
        white[w] = (transform * (lax.rsqrt(band_power + epsilon) * usable)).astype(jnp.bfloat16)

    mix_load.wait()
    pair = 16 // (2 * windows)
    bins = mix_ref.shape[0] // (2 * windows)
    groups = bins // pair
    for block in range(F // bins):
        parts = [
            white[v, p * F + block * bins : p * F + (block + 1) * bins, :] for v in range(windows) for p in range(2)
        ]
        product = jnp.dot(mix_ref[...], jnp.concatenate(parts, 0), preferred_element_type=jnp.float32)
        mixed[block * groups : (block + 1) * groups] = product.astype(jnp.bfloat16).reshape(groups, 16, width)
    me = lax.axis_index("win")
    chip, core = me // 2, me % 2
    chips, share = keep_ref.shape[:2]
    for k in range(chips):
        at = (chip ^ k) * 2 * share
        keep_ref[k] = mixed[pl.ds(at + core * share, share)]
        give_ref[k] = mixed[pl.ds(at + (1 - core) * share, share)]


def in_vmem(count):
    return [pl.BlockSpec(memory_space=pltpu.VMEM)] * count


def spectra(raw, offsets, quality, table, mix, dests):
    windows, _, width = raw.shape
    groups = F * 2 * windows // 16
    blocks = (dests // 2, groups // dests, 16, width)
    return pl.pallas_call(
        spectra_kernel,
        in_specs=[pl.BlockSpec(memory_space=pltpu.SMEM)] + [pl.BlockSpec(memory_space=pl.ANY)] * 4,
        out_specs=in_vmem(2),
        scratch_shapes=[
            pltpu.VMEM(table.shape, table.dtype),
            pltpu.VMEM(mix.shape, mix.dtype),
            pltpu.VMEM(quality.shape, quality.dtype),
            pltpu.VMEM(raw.shape, raw.dtype),
            pltpu.VMEM((windows, 2 * F, width), jnp.bfloat16),
            pltpu.VMEM((groups, 16, width), jnp.bfloat16),
            pltpu.SemaphoreType.DMA((windows + 3,)),
            *[pltpu.VMEM((L, width), jnp.bfloat16)] * windows,
        ],
        out_shape=[jax.ShapeDtypeStruct(blocks, jnp.bfloat16)] * 2,
        compiler_params=pltpu.CompilerParams(vmem_limit_bytes=SPECTRA_MIB * MIB),
        cost_estimate=pl.CostEstimate(
            flops=2 * windows * 2 * F * L * width, bytes_accessed=2 * windows * raw.shape[1] * width + 4 * F * L, transcendentals=0
        ),
        name="spectra",
    )(offsets, table, mix, raw, quality)


def join_kernel(moves, *refs):
    out_ref = refs[-1]
    groups = out_ref.shape[1]
    to = 0
    for i, at, source, count in moves:
        out_ref[to : to + count] = refs[i][source : source + count, at : at + groups]
        to += count


def join(views, groups):
    arrays, moves = [], []
    for x, *where in views:
        known = [i for i, y in enumerate(arrays) if y is x]
        if not known:
            arrays.append(x)
        moves.append((known[0] if known else len(arrays) - 1, *where))
    shape = (sum(move[3] for move in moves), groups, *arrays[0].shape[2:])
    return pl.pallas_call(
        functools.partial(join_kernel, moves),
        in_specs=in_vmem(len(arrays)),
        out_specs=in_vmem(1)[0],
        out_shape=jax.ShapeDtypeStruct(shape, arrays[0].dtype),
        compiler_params=pltpu.CompilerParams(vmem_limit_bytes=12 * MIB),
        cost_estimate=pl.CostEstimate(flops=0, bytes_accessed=4 * math.prod(shape), transcendentals=0),
        name="join",
    )(*arrays)


def view(ref, group, at, sources):
    return ref[sources[0] : sources[1], group - at].reshape(-1, ref.shape[-1])


def turn_kernel(first_group, views, *refs):
    out_ref = refs[-1]
    _, _, width, depth = out_ref.shape

    def body(g, carry):
        x = jnp.concatenate([view(refs[i], first_group + g, *where) for i, where in enumerate(views)], 0)
        by_part = x.astype(jnp.float32).reshape(depth // 16, 16, width)
        turned = jnp.concatenate([by_part[:, 8:], -by_part[:, :8]], 1)
        out_ref[g, 0] = by_part.reshape(depth, width).T.astype(jnp.bfloat16)
        out_ref[g, 1] = turned.reshape(depth, width).T.astype(jnp.bfloat16)
        return carry

    lax.fori_loop(0, out_ref.shape[0], body, 0)


def turn(items, first_group, groups):
    rows, width = items[0][0].shape[2:]
    depth = sum(sources[1] - sources[0] for _, _, sources in items) * rows
    return pl.pallas_call(
        functools.partial(turn_kernel, first_group, [item[1:] for item in items]),
        in_specs=in_vmem(len(items)),
        out_specs=in_vmem(1)[0],
        out_shape=jax.ShapeDtypeStruct((groups, 2, width, depth), jnp.bfloat16),
        compiler_params=pltpu.CompilerParams(vmem_limit_bytes=12 * MIB),
        cost_estimate=pl.CostEstimate(flops=0, bytes_accessed=8 * groups * width * depth, transcendentals=0),
        name="turn",
    )(*[item[0] for item in items])


def closed_walk(i, members):
    return jnp.where(i < members // 2, i, members - 1 - i + members // 2)


def stack_kernel(windows, scale, first_group, layout, left_ref, *refs):
    out_ref = refs[-1]
    pair = 16 // (2 * windows)
    width, depth = left_ref.shape[2:]
    step_groups = out_ref.shape[0] // pair
    members = len(layout)
    where = closed_walk(lax.axis_index("chan"), members)
    bin_of = lax.broadcasted_iota(jnp.int32, (width, depth), 1) % 8 // windows
    masks = [jnp.where(bin_of == b, 1.0, 0.0).astype(jnp.bfloat16) for b in range(pair)]
    for s in range(step_groups):
        g = pl.program_id(0) * step_groups + s
        sides = [left_ref[g, part] for part in range(2)]
        for step, items in layout:
            right = jnp.concatenate([view(refs[i], first_group + g, *item) for i, item in items], 0)
            column = closed_walk(lax.rem(where + (step + members), members), members)
            columns = pl.ds(pl.multiple_of(column * width, width), width)
            for b in range(pair):
                for part in range(2):
                    product = jnp.dot(sides[part] * masks[b], right, preferred_element_type=jnp.float32)
                    out_ref[s * pair + b, part, :, columns] = (product * scale).astype(jnp.bfloat16)


def stack(left, steps, into, first_group, bins, windows, sources):
    members = len(steps)
    groups, _, width, depth = left.shape
    pair = 16 // (2 * windows)
    step_groups = max(n for n in range(1, STEP_GROUPS + 1) if groups % n == 0 and first_group % n == 0)
    operands, layout = [left], []
    for step, items in steps:
        layout.append((step, [(len(operands) - 1 + i, item[1:]) for i, item in enumerate(items)]))
        operands += [item[0] for item in items]
    in_specs = in_vmem(len(operands))
    aliases = {}
    if into is not None:
        aliases = {len(operands): 0}
        operands.append(into)
        in_specs.append(pl.BlockSpec(memory_space=pl.ANY))
    block = (step_groups * pair, 2, width, members * width)
    return pl.pallas_call(
        functools.partial(stack_kernel, windows, 1.0 / math.sqrt(sources), first_group, layout),
        grid=(groups // step_groups,),
        in_specs=in_specs,
        out_specs=pl.BlockSpec(block, lambda g: (first_group // step_groups + g, 0, 0, 0)),
        out_shape=jax.ShapeDtypeStruct((bins, 2, width, members * width), jnp.bfloat16),
        input_output_aliases=aliases,
        compiler_params=pltpu.CompilerParams(vmem_limit_bytes=24 * MIB, dimension_semantics=("arbitrary",)),
        cost_estimate=pl.CostEstimate(
            flops=4 * groups * pair * depth * width * width * members,
            bytes_accessed=4 * groups * pair * width * members * width,
            transcendentals=0,
        ),
        name="stack",
    )(*operands)


def after(arrays, *earlier):
    return list(lax.optimization_barrier((tuple(arrays), earlier))[0])


def ring_walk(members):
    ring = [i if i < members // 2 else members - 1 - i + members // 2 for i in range(members)]
    return [(ring[i], ring[(i + 1) % members]) for i in range(members)]


def ring_start(x, members):
    ahead = ring_walk(members)
    back = [(b, a) for a, b in ahead]
    left = right = x
    blocks = [(0, [x])]
    for step in range(1, (members + 1) // 2):
        left = lax.ppermute(left, "chan", ahead)
        right = lax.ppermute(right, "chan", back)
        blocks += [(-step, [left]), (step, [right])]
    return blocks


def ring_finish(blocks, members, *earlier):
    if members % 2:
        return blocks
    ahead = ring_walk(members)
    left, right = blocks[-2][1][0], blocks[-1][1][0]
    if earlier:
        left, right = after((left, right), *earlier)
    cut_at = left.shape[0] // 2
    first = lax.ppermute(left[:cut_at], "chan", ahead)
    second = lax.ppermute(right[cut_at:], "chan", [(b, a) for a, b in ahead])
    return blocks + [(members // 2, [first, second])]


def neighbours(blocks):
    return [array for step, arrays in blocks if step for array in arrays]


def local(dests, members, raw, offsets, quality):
    windows = raw.shape[0]
    pair = 16 // (2 * windows)
    bins = F // dests
    share = bins // pair
    chips = dests // 2
    assert chips & (chips - 1) == 0
    table = jnp.asarray(dft_table())
    mix = jnp.asarray(interleave(windows, 256 // (2 * windows)))

    keep, give = spectra(raw, offsets, quality, table, mix, dests)
    other = lax.ppermute(give, "win", [(i, i ^ 1) for i in range(dests)])
    own = join([(keep, 0, 0, 1), (other, 0, 0, 1)], share)
    begun = [ring_start(own, members)]
    came = []
    for k in range(1, chips):
        sent = join([(keep, 0, k, 1), (other, 0, k, 1)], share)
        if k > 2:
            sent = after([sent], came[k - 3])[0]
        came.append(lax.ppermute(sent, "win", [(i, i ^ (2 * k)) for i in range(dests)]))

    units = [(own, 0, share)]
    units += [(x, 0, share) for x in came[:-1]]
    cuts = [share * i // UNITS for i in range(UNITS + 1)]
    for low, high in zip(cuts[:-1], cuts[1:]):
        if low < high:
            units.append((join([(came[-1], low, 0, 2)], high - low), low, high))
    done = []
    out = None
    for n, (x, low, high) in enumerate(units):
        if n > 0:
            earlier = neighbours(begun[n - 1])
            if n > 1:
                earlier += neighbours(done[n - 2][-1:])
            begun.append(ring_start(after([x], *earlier)[0], members))
        done.append(ring_finish(begun[n], members))
        if high - low == share and n + 1 < len(units):
            continue
        parts = [m for m in range(n + 1) if units[m][1] <= low and high <= units[m][2]]
        steps = []
        for same in zip(*[done[m] for m in parts]):
            views = [(x, units[m][1], (0, x.shape[0])) for m, (_, arrays) in zip(parts, same) for x in arrays]
            steps.append((same[0][0], views))
        left = turn(steps[0][1], low, high - low)
        out = stack(left, steps, out, low, bins, windows, dests * windows)
    return out


def solution(mesh):
    in_specs = (P("win", None, "chan"), P("win"), P("win", "chan"))
    out_specs = P("win", None, "chan", None)
    run = functools.partial(local, mesh.shape["win"], mesh.shape["chan"])
    return jax.shard_map(run, mesh=mesh, in_specs=in_specs, out_specs=out_specs, check_vma=False)
```

```python
import functools
import math

import jax
import jax.numpy as jnp
import ml_dtypes
import numpy as np
from jax import lax
from jax.experimental import pallas as pl
from jax.experimental.pallas import tpu as pltpu
from jax.sharding import PartitionSpec as P

F = 384
L = 3072
FIRST_BIN = 60
CHUNK_WEIGHTS = (1, 1, 1)
STEP_GROUPS = 2
SPECTRA_MIB = 50

epsilon = 1e-05
MIB = 1024 * 1024


def dft_table():
    sample_idx = np.arange(L, dtype=np.int64)
    bin_idx = FIRST_BIN + np.arange(F, dtype=np.int64)
    residue = bin_idx[:, None] * sample_idx[None, :] % L
    angles = residue.astype(np.float32) * np.float32(2.0 * math.pi / L)
    return np.concatenate([np.cos(angles), -np.sin(angles)], 0).astype(ml_dtypes.bfloat16)


def interleave(windows, bins):
    pair = 16 // (2 * windows)
    out = np.zeros((2 * windows * bins, 2 * windows * bins), np.float32)
    for f in range(bins):
        for p in range(2):
            for w in range(windows):
                row = ((f // pair * 2 + p) * pair + f % pair) * windows + w
                out[row, (w * 2 + p) * bins + f] = 1.0
    return out.astype(ml_dtypes.bfloat16)


def cut(raw_ref, slot, shift_at, window_ref):
    width = raw_ref.shape[2]
    spare = raw_ref.shape[1] - L
    tile = 256
    base = jnp.minimum(shift_at // 16, (spare - 16) // 16) * 16
    rest = shift_at - base
    whole = rest // 8
    fine = rest - whole * 8
    back = jnp.where(fine == 0, 0, 8 - fine)
    keep = lax.broadcasted_iota(jnp.int32, (tile // 8, 8, width), 1) < 8 - fine
    count = tile // 8
    for step in range(L // tile):
        start = pl.multiple_of(base + step * tile, 16)
        rows = raw_ref[slot, pl.ds(start, tile + 16), :].astype(jnp.float32).reshape(count + 2, 8, width)
        rolled = pltpu.roll(rows, back, 1)
        upper = jnp.where(whole == 0, rolled[1 : count + 1], rolled[2:])
        lower = jnp.where(whole == 0, rolled[:count], jnp.where(whole == 1, rolled[1 : count + 1], rolled[2:]))
        moved = jnp.where(keep, lower, upper)
        window_ref[step * tile : (step + 1) * tile, :] = moved.reshape(tile, width).astype(jnp.bfloat16)


def spectra_kernel(offsets_ref, table_hbm, mix_hbm, raw_hbm, quality_hbm, keep_ref, give_ref, *scratch):
    table_ref, mix_ref, quality_ref, raw_ref, white, mixed, sems = scratch[:7]
    cuts = scratch[7:]
    windows, _, width = raw_ref.shape
    loads = [pltpu.make_async_copy(raw_hbm.at[w], raw_ref.at[w], sems.at[w]) for w in range(windows)]
    table_load = pltpu.make_async_copy(table_hbm, table_ref, sems.at[windows])
    mix_load = pltpu.make_async_copy(mix_hbm, mix_ref, sems.at[windows + 1])
    quality_load = pltpu.make_async_copy(quality_hbm, quality_ref, sems.at[windows + 2])
    for load in (loads[0], table_load, *loads[1:], quality_load, mix_load):
        load.start()
    loads[0].wait()
    cut(raw_ref, 0, offsets_ref[0], cuts[0])
    for load in (table_load, *loads[1:], quality_load, mix_load):
        load.wait()
    for w in range(windows):
        if w + 1 < windows:
            cut(raw_ref, w + 1, offsets_ref[w + 1], cuts[w + 1])
        transform = jnp.dot(table_ref[...], cuts[w][...], preferred_element_type=jnp.float32)
        band_power = jnp.sum(transform * transform, axis=0, keepdims=True) / F
        usable = quality_ref[w : w + 1, :].astype(jnp.float32)
        white[w] = (transform * (lax.rsqrt(band_power + epsilon) * usable)).astype(jnp.bfloat16)

    pair = 16 // (2 * windows)
    bins = mix_ref.shape[0] // (2 * windows)
    groups = bins // pair
    for block in range(F // bins):
        parts = [
            white[v, p * F + block * bins : p * F + (block + 1) * bins, :] for v in range(windows) for p in range(2)
        ]
        product = jnp.dot(mix_ref[...], jnp.concatenate(parts, 0), preferred_element_type=jnp.float32)
        mixed[block * groups : (block + 1) * groups] = product.astype(jnp.bfloat16).reshape(groups, 16, width)
    me = lax.axis_index("win")
    chip, core = me // 2, me % 2
    chips, share = keep_ref.shape[:2]
    for k in range(chips):
        at = (chip ^ k) * 2 * share
        keep_ref[k] = mixed[pl.ds(at + core * share, share)]
        give_ref[k] = mixed[pl.ds(at + (1 - core) * share, share)]


def in_vmem(count):
    return [pl.BlockSpec(memory_space=pltpu.VMEM)] * count


def spectra(raw, offsets, quality, table, mix, dests):
    windows, _, width = raw.shape
    groups = F * 2 * windows // 16
    blocks = (dests // 2, groups // dests, 16, width)
    return pl.pallas_call(
        spectra_kernel,
        in_specs=[pl.BlockSpec(memory_space=pltpu.SMEM)] + [pl.BlockSpec(memory_space=pl.ANY)] * 4,
        out_specs=in_vmem(2),
        scratch_shapes=[
            pltpu.VMEM(table.shape, table.dtype),
            pltpu.VMEM(mix.shape, mix.dtype),
            pltpu.VMEM(quality.shape, quality.dtype),
            pltpu.VMEM(raw.shape, raw.dtype),
            pltpu.VMEM((windows, 2 * F, width), jnp.bfloat16),
            pltpu.VMEM((groups, 16, width), jnp.bfloat16),
            pltpu.SemaphoreType.DMA((windows + 3,)),
            *[pltpu.VMEM((L, width), jnp.bfloat16)] * windows,
        ],
        out_shape=[jax.ShapeDtypeStruct(blocks, jnp.bfloat16)] * 2,
        compiler_params=pltpu.CompilerParams(vmem_limit_bytes=SPECTRA_MIB * MIB),
        cost_estimate=pl.CostEstimate(
            flops=2 * windows * 2 * F * L * width, bytes_accessed=2 * windows * raw.shape[1] * width + 4 * F * L, transcendentals=0
        ),
        name="spectra",
    )(offsets, table, mix, raw, quality)


def join_kernel(moves, *refs):
    out_ref = refs[-1]
    groups = out_ref.shape[1]
    to = 0
    for i, at, source, count in moves:
        out_ref[to : to + count] = refs[i][source : source + count, at : at + groups]
        to += count


def join(views, groups):
    arrays, moves = [], []
    for x, *where in views:
        known = [i for i, y in enumerate(arrays) if y is x]
        if not known:
            arrays.append(x)
        moves.append((known[0] if known else len(arrays) - 1, *where))
    shape = (sum(move[3] for move in moves), groups, *arrays[0].shape[2:])
    return pl.pallas_call(
        functools.partial(join_kernel, moves),
        in_specs=in_vmem(len(arrays)),
        out_specs=in_vmem(1)[0],
        out_shape=jax.ShapeDtypeStruct(shape, arrays[0].dtype),
        compiler_params=pltpu.CompilerParams(vmem_limit_bytes=12 * MIB),
        cost_estimate=pl.CostEstimate(flops=0, bytes_accessed=4 * math.prod(shape), transcendentals=0),
        name="join",
    )(*arrays)


def view(ref, group, at, sources):
    return ref[sources[0] : sources[1], group - at].reshape(-1, ref.shape[-1])


def turn_kernel(first_group, views, *refs):
    out_ref = refs[-1]
    _, _, width, depth = out_ref.shape

    def body(g, carry):
        x = jnp.concatenate([view(refs[i], first_group + g, *where) for i, where in enumerate(views)], 0)
        by_part = x.astype(jnp.float32).reshape(depth // 16, 16, width)
        turned = jnp.concatenate([by_part[:, 8:], -by_part[:, :8]], 1)
        out_ref[g, 0] = by_part.reshape(depth, width).T.astype(jnp.bfloat16)
        out_ref[g, 1] = turned.reshape(depth, width).T.astype(jnp.bfloat16)
        return carry

    lax.fori_loop(0, out_ref.shape[0], body, 0)


def turn(items, first_group, groups):
    rows, width = items[0][0].shape[2:]
    depth = sum(sources[1] - sources[0] for _, _, sources in items) * rows
    return pl.pallas_call(
        functools.partial(turn_kernel, first_group, [item[1:] for item in items]),
        in_specs=in_vmem(len(items)),
        out_specs=in_vmem(1)[0],
        out_shape=jax.ShapeDtypeStruct((groups, 2, width, depth), jnp.bfloat16),
        compiler_params=pltpu.CompilerParams(vmem_limit_bytes=12 * MIB),
        cost_estimate=pl.CostEstimate(flops=0, bytes_accessed=8 * groups * width * depth, transcendentals=0),
        name="turn",
    )(*[item[0] for item in items])


def closed_walk(i, members):
    return jnp.where(i < members // 2, i, members - 1 - i + members // 2)


def stack_kernel(windows, scale, first_group, layout, left_ref, *refs):
    out_ref = refs[-1]
    pair = 16 // (2 * windows)
    width, depth = left_ref.shape[2:]
    step_groups = out_ref.shape[0] // pair
    members = len(layout)
    where = closed_walk(lax.axis_index("chan"), members)
    bin_of = lax.broadcasted_iota(jnp.int32, (width, depth), 1) % 8 // windows
    masks = [jnp.where(bin_of == b, 1.0, 0.0).astype(jnp.bfloat16) for b in range(pair)]
    for s in range(step_groups):
        g = pl.program_id(0) * step_groups + s
        sides = [left_ref[g, part] for part in range(2)]
        for step, items in layout:
            right = jnp.concatenate([view(refs[i], first_group + g, *item) for i, item in items], 0)
            column = closed_walk(lax.rem(where + (step + members), members), members)
            columns = pl.ds(pl.multiple_of(column * width, width), width)
            for b in range(pair):
                for part in range(2):
                    product = jnp.dot(sides[part] * masks[b], right, preferred_element_type=jnp.float32)
                    out_ref[s * pair + b, part, :, columns] = (product * scale).astype(jnp.bfloat16)


def stack(left, steps, into, first_group, bins, windows, sources):
    members = len(steps)
    groups, _, width, depth = left.shape
    pair = 16 // (2 * windows)
    step_groups = max(n for n in range(1, STEP_GROUPS + 1) if groups % n == 0 and first_group % n == 0)
    operands, layout = [left], []
    for step, items in steps:
        layout.append((step, [(len(operands) - 1 + i, item[1:]) for i, item in enumerate(items)]))
        operands += [item[0] for item in items]
    in_specs = in_vmem(len(operands))
    aliases = {}
    if into is not None:
        aliases = {len(operands): 0}
        operands.append(into)
        in_specs.append(pl.BlockSpec(memory_space=pl.ANY))
    block = (step_groups * pair, 2, width, members * width)
    return pl.pallas_call(
        functools.partial(stack_kernel, windows, 1.0 / math.sqrt(sources), first_group, layout),
        grid=(groups // step_groups,),
        in_specs=in_specs,
        out_specs=pl.BlockSpec(block, lambda g: (first_group // step_groups + g, 0, 0, 0)),
        out_shape=jax.ShapeDtypeStruct((bins, 2, width, members * width), jnp.bfloat16),
        input_output_aliases=aliases,
        compiler_params=pltpu.CompilerParams(vmem_limit_bytes=24 * MIB, dimension_semantics=("arbitrary",)),
        cost_estimate=pl.CostEstimate(
            flops=4 * groups * pair * depth * width * width * members,
            bytes_accessed=4 * groups * pair * width * members * width,
            transcendentals=0,
        ),
        name="stack",
    )(*operands)


def after(arrays, *earlier):
    return list(lax.optimization_barrier((tuple(arrays), earlier))[0])


def ring_walk(members):
    ring = [i if i < members // 2 else members - 1 - i + members // 2 for i in range(members)]
    return [(ring[i], ring[(i + 1) % members]) for i in range(members)]


def ring_start(x, members):
    ahead = ring_walk(members)
    back = [(b, a) for a, b in ahead]
    left = right = x
    blocks = [(0, [x])]
    for step in range(1, (members + 1) // 2):
        left = lax.ppermute(left, "chan", ahead)
        right = lax.ppermute(right, "chan", back)
        blocks += [(-step, [left]), (step, [right])]
    return blocks


def ring_finish(blocks, members, *earlier):
    if members % 2:
        return blocks
    ahead = ring_walk(members)
    left, right = blocks[-2][1][0], blocks[-1][1][0]
    if earlier:
        left, right = after((left, right), *earlier)
    cut_at = left.shape[0] // 2
    first = lax.ppermute(left[:cut_at], "chan", ahead)
    second = lax.ppermute(right[cut_at:], "chan", [(b, a) for a, b in ahead])
    return blocks + [(members // 2, [first, second])]


def neighbours(blocks):
    return [array for step, arrays in blocks if step for array in arrays]


def chunk_starts(share):
    total, starts, seen = sum(CHUNK_WEIGHTS), [0], 0
    for weight in CHUNK_WEIGHTS:
        seen += weight
        starts.append(round(share * seen / total))
    return starts


def local(dests, members, raw, offsets, quality):
    windows = raw.shape[0]
    pair = 16 // (2 * windows)
    bins = F // dests
    share = bins // pair
    chips = dests // 2
    assert chips & (chips - 1) == 0
    starts = chunk_starts(share)
    chunks = list(zip(starts[:-1], starts[1:]))
    table = jnp.asarray(dft_table())
    mix = jnp.asarray(interleave(windows, 256 // (2 * windows)))

    keep, give = spectra(raw, offsets, quality, table, mix, dests)
    other = lax.ppermute(give, "win", [(i, i ^ 1) for i in range(dests)])
    own = join([(keep, 0, 0, 1), (other, 0, 0, 1)], share)
    own_start = ring_start(own, members)
    own_blocks = ring_finish(own_start, members)

    pieces = []
    for start, stop in chunks:
        came = []
        for k in range(1, chips):
            sent = join([(keep, start, k, 1), (other, start, k, 1)], stop - start)
            if pieces:
                sent = after([sent], *neighbours(own_start), pieces[-1][0])[0]
            came.append(lax.ppermute(sent, "win", [(i, i ^ (2 * k)) for i in range(dests)]))
        pieces.append(came)

    out = None
    for n, ((start, stop), came) in enumerate(zip(chunks, pieces)):
        far = join([(x, 0, 0, 2) for x in came], stop - start)
        begun = ring_start(far, members)
        blocks = ring_finish(begun, members, *([] if out is None else [out]))
        steps = []
        for (step, own_arrays), (_, arrays) in zip(own_blocks, blocks):
            views = [(x, 0, (0, x.shape[0])) for x in own_arrays] + [(x, start, (0, x.shape[0])) for x in arrays]
            steps.append((step, views))
        left = turn(steps[0][1], start, stop - start)
        out = stack(left, steps, out, start, bins, windows, dests * windows)
    return out


def solution(mesh):
    in_specs = (P("win", None, "chan"), P("win"), P("win", "chan"))
    out_specs = P("win", None, "chan", None)
    run = functools.partial(local, mesh.shape["win"], mesh.shape["chan"])
    return jax.shard_map(run, mesh=mesh, in_specs=in_specs, out_specs=out_specs, check_vma=False)
```

```python
import functools
import math

import jax
import jax.numpy as jnp
import ml_dtypes
import numpy as np
from jax import lax
from jax.experimental import pallas as pl
from jax.experimental.pallas import tpu as pltpu
from jax.sharding import PartitionSpec as P

F = 384
L = 3072
FIRST_BIN = 60
CHUNK_WEIGHTS = (1, 1, 1)
STEP_GROUPS = 2
SPECTRA_MIB = 50

epsilon = 1e-05
MIB = 1024 * 1024


def dft_table():
    sample_idx = np.arange(L, dtype=np.int64)
    bin_idx = FIRST_BIN + np.arange(F, dtype=np.int64)
    residue = bin_idx[:, None] * sample_idx[None, :] % L
    angles = residue.astype(np.float32) * np.float32(2.0 * math.pi / L)
    return np.concatenate([np.cos(angles), -np.sin(angles)], 0).astype(ml_dtypes.bfloat16)


def interleave(windows, bins):
    pair = 16 // (2 * windows)
    rows = 2 * windows * bins
    row = lax.broadcasted_iota(jnp.int32, (rows, rows), 0)
    col = lax.broadcasted_iota(jnp.int32, (rows, rows), 1)
    w, b, p, g = row % windows, row // windows % pair, row // 8 % 2, row // 16
    return jnp.where(col == (w * 2 + p) * bins + g * pair + b, 1.0, 0.0).astype(jnp.bfloat16)


def cut(raw_ref, slot, shift_at, window_ref):
    width = raw_ref.shape[2]
    spare = raw_ref.shape[1] - L
    tile = 256
    base = jnp.minimum(shift_at // 16, (spare - 16) // 16) * 16
    rest = shift_at - base
    whole = rest // 8
    fine = rest - whole * 8
    back = jnp.where(fine == 0, 0, 8 - fine)
    keep = lax.broadcasted_iota(jnp.int32, (tile // 8, 8, width), 1) < 8 - fine
    count = tile // 8
    for step in range(L // tile):
        start = pl.multiple_of(base + step * tile, 16)
        rows = raw_ref[slot, pl.ds(start, tile + 16), :].astype(jnp.float32).reshape(count + 2, 8, width)
        rolled = pltpu.roll(rows, back, 1)
        upper = jnp.where(whole == 0, rolled[1 : count + 1], rolled[2:])
        lower = jnp.where(whole == 0, rolled[:count], jnp.where(whole == 1, rolled[1 : count + 1], rolled[2:]))
        moved = jnp.where(keep, lower, upper)
        window_ref[step * tile : (step + 1) * tile, :] = moved.reshape(tile, width).astype(jnp.bfloat16)


def spectra_kernel(offsets_ref, table_hbm, raw_hbm, quality_hbm, keep_ref, give_ref, *scratch):
    table_ref, quality_ref, raw_ref, white, mixed, sems = scratch[:6]
    cuts = scratch[6:]
    windows, _, width = raw_ref.shape
    loads = [pltpu.make_async_copy(raw_hbm.at[w], raw_ref.at[w], sems.at[w]) for w in range(windows)]
    table_load = pltpu.make_async_copy(table_hbm, table_ref, sems.at[windows])
    quality_load = pltpu.make_async_copy(quality_hbm, quality_ref, sems.at[windows + 1])
    for load in (loads[0], quality_load, table_load, *loads[1:]):
        load.start()
    loads[0].wait()
    cut(raw_ref, 0, offsets_ref[0], cuts[0])
    mix = interleave(windows, 256 // (2 * windows))
    quality_load.wait()
    table_load.wait()
    for w in range(windows):
        if w + 1 < windows:
            loads[w + 1].wait()
            cut(raw_ref, w + 1, offsets_ref[w + 1], cuts[w + 1])
        transform = jnp.dot(table_ref[...], cuts[w][...], preferred_element_type=jnp.float32)
        band_power = jnp.sum(transform * transform, axis=0, keepdims=True) / F
        usable = quality_ref[w : w + 1, :].astype(jnp.float32)
        white[w] = (transform * (lax.rsqrt(band_power + epsilon) * usable)).astype(jnp.bfloat16)

    pair = 16 // (2 * windows)
    bins = mix.shape[0] // (2 * windows)
    groups = bins // pair
    for block in range(F // bins):
        parts = [
            white[v, p * F + block * bins : p * F + (block + 1) * bins, :] for v in range(windows) for p in range(2)
        ]
        product = jnp.dot(mix, jnp.concatenate(parts, 0), preferred_element_type=jnp.float32)
        mixed[block * groups : (block + 1) * groups] = product.astype(jnp.bfloat16).reshape(groups, 16, width)
    me = lax.axis_index("win")
    chip, core = me // 2, me % 2
    chips, share = keep_ref.shape[:2]
    for k in range(chips):
        at = (chip ^ k) * 2 * share
        keep_ref[k] = mixed[pl.ds(at + core * share, share)]
        give_ref[k] = mixed[pl.ds(at + (1 - core) * share, share)]


def in_vmem(count):
    return [pl.BlockSpec(memory_space=pltpu.VMEM)] * count


def spectra(raw, offsets, quality, table, dests):
    windows, _, width = raw.shape
    groups = F * 2 * windows // 16
    blocks = (dests // 2, groups // dests, 16, width)
    return pl.pallas_call(
        spectra_kernel,
        in_specs=[pl.BlockSpec(memory_space=pltpu.SMEM)] + [pl.BlockSpec(memory_space=pl.ANY)] * 3,
        out_specs=in_vmem(2),
        scratch_shapes=[
            pltpu.VMEM(table.shape, table.dtype),
            pltpu.VMEM(quality.shape, quality.dtype),
            pltpu.VMEM(raw.shape, raw.dtype),
            pltpu.VMEM((windows, 2 * F, width), jnp.bfloat16),
            pltpu.VMEM((groups, 16, width), jnp.bfloat16),
            pltpu.SemaphoreType.DMA((windows + 2,)),
            *[pltpu.VMEM((L, width), jnp.bfloat16)] * windows,
        ],
        out_shape=[jax.ShapeDtypeStruct(blocks, jnp.bfloat16)] * 2,
        compiler_params=pltpu.CompilerParams(vmem_limit_bytes=SPECTRA_MIB * MIB),
        cost_estimate=pl.CostEstimate(
            flops=2 * windows * 2 * F * L * width, bytes_accessed=2 * windows * raw.shape[1] * width + 4 * F * L, transcendentals=0
        ),
        name="spectra",
    )(offsets, table, raw, quality)


def join_kernel(moves, *refs):
    out_ref = refs[-1]
    groups = out_ref.shape[1]
    to = 0
    for i, at, source, count in moves:
        out_ref[to : to + count] = refs[i][source : source + count, at : at + groups]
        to += count


def join(views, groups):
    arrays, moves = [], []
    for x, *where in views:
        known = [i for i, y in enumerate(arrays) if y is x]
        if not known:
            arrays.append(x)
        moves.append((known[0] if known else len(arrays) - 1, *where))
    shape = (sum(move[3] for move in moves), groups, *arrays[0].shape[2:])
    return pl.pallas_call(
        functools.partial(join_kernel, moves),
        in_specs=in_vmem(len(arrays)),
        out_specs=in_vmem(1)[0],
        out_shape=jax.ShapeDtypeStruct(shape, arrays[0].dtype),
        compiler_params=pltpu.CompilerParams(vmem_limit_bytes=12 * MIB),
        cost_estimate=pl.CostEstimate(flops=0, bytes_accessed=4 * math.prod(shape), transcendentals=0),
        name="join",
    )(*arrays)


def view(ref, group, at, sources):
    return ref[sources[0] : sources[1], group - at].reshape(-1, ref.shape[-1])


def turn_kernel(windows, first_group, views, *refs):
    out_ref = refs[-1]
    _, pair, _, width, depth = out_ref.shape
    bin_of = lax.broadcasted_iota(jnp.int32, (width, depth), 1) % 8 // windows

    def body(g, carry):
        x = jnp.concatenate([view(refs[i], first_group + g, *where) for i, where in enumerate(views)], 0)
        by_part = x.astype(jnp.float32).reshape(depth // 16, 16, width)
        turned = jnp.concatenate([by_part[:, 8:], -by_part[:, :8]], 1)
        for part, rows in enumerate((by_part, turned)):
            left = rows.reshape(depth, width).T
            for b in range(pair):
                out_ref[g, b, part] = jnp.where(bin_of == b, left, 0.0).astype(jnp.bfloat16)
        return carry

    lax.fori_loop(0, out_ref.shape[0], body, 0)


def turn(items, first_group, groups, windows):
    rows, width = items[0][0].shape[2:]
    depth = sum(sources[1] - sources[0] for _, _, sources in items) * rows
    pair = 16 // (2 * windows)
    return pl.pallas_call(
        functools.partial(turn_kernel, windows, first_group, [item[1:] for item in items]),
        in_specs=in_vmem(len(items)),
        out_specs=in_vmem(1)[0],
        out_shape=jax.ShapeDtypeStruct((groups, pair, 2, width, depth), jnp.bfloat16),
        compiler_params=pltpu.CompilerParams(vmem_limit_bytes=12 * MIB),
        cost_estimate=pl.CostEstimate(flops=0, bytes_accessed=8 * groups * width * depth, transcendentals=0),
        name="turn",
    )(*[item[0] for item in items])


def closed_walk(i, members):
    return jnp.where(i < members // 2, i, members - 1 - i + members // 2)


def stack_kernel(scale, left_first, first_group, layout, left_ref, *refs):
    out_ref = refs[-1]
    pair, _, width, _ = left_ref.shape[1:]
    step_groups = out_ref.shape[0] // pair
    members = len(layout)
    where = closed_walk(lax.axis_index("chan"), members)
    for s in range(step_groups):
        g = pl.program_id(0) * step_groups + s
        for step, items in layout:
            right = jnp.concatenate([view(refs[i], first_group + g, *item) for i, item in items], 0)
            column = closed_walk(lax.rem(where + (step + members), members), members)
            columns = pl.ds(pl.multiple_of(column * width, width), width)
            for b in range(pair):
                for part in range(2):
                    left = left_ref[first_group - left_first + g, b, part]
                    product = jnp.dot(left, right, preferred_element_type=jnp.float32)
                    out_ref[s * pair + b, part, :, columns] = (product * scale).astype(jnp.bfloat16)


def stack(left, left_first, steps, into, first_group, groups, bins, sources):
    members = len(steps)
    _, pair, _, width, depth = left.shape
    step_groups = max(n for n in range(1, STEP_GROUPS + 1) if groups % n == 0 and first_group % n == 0)
    operands, layout = [left], []
    for step, items in steps:
        layout.append((step, [(len(operands) - 1 + i, item[1:]) for i, item in enumerate(items)]))
        operands += [item[0] for item in items]
    in_specs = in_vmem(len(operands))
    aliases = {}
    if into is not None:
        aliases = {len(operands): 0}
        operands.append(into)
        in_specs.append(pl.BlockSpec(memory_space=pl.ANY))
    block = (step_groups * pair, 2, width, members * width)
    return pl.pallas_call(
        functools.partial(stack_kernel, 1.0 / math.sqrt(sources), left_first, first_group, layout),
        grid=(groups // step_groups,),
        in_specs=in_specs,
        out_specs=pl.BlockSpec(block, lambda g: (first_group // step_groups + g, 0, 0, 0)),
        out_shape=jax.ShapeDtypeStruct((bins, 2, width, members * width), jnp.bfloat16),
        input_output_aliases=aliases,
        compiler_params=pltpu.CompilerParams(vmem_limit_bytes=24 * MIB, dimension_semantics=("arbitrary",)),
        cost_estimate=pl.CostEstimate(
            flops=4 * groups * pair * depth * width * width * members,
            bytes_accessed=4 * groups * pair * width * members * width,
            transcendentals=0,
        ),
        name="stack",
    )(*operands)


def after(arrays, *earlier):
    return list(lax.optimization_barrier((tuple(arrays), earlier))[0])


def ring_walk(members):
    ring = [i if i < members // 2 else members - 1 - i + members // 2 for i in range(members)]
    return [(ring[i], ring[(i + 1) % members]) for i in range(members)]


def ring_start(x, members):
    ahead = ring_walk(members)
    back = [(b, a) for a, b in ahead]
    left = right = x
    blocks = [(0, [x])]
    for step in range(1, (members + 1) // 2):
        left = lax.ppermute(left, "chan", ahead)
        right = lax.ppermute(right, "chan", back)
        blocks += [(-step, [left]), (step, [right])]
    return blocks


def ring_finish(blocks, members, *earlier):
    if members % 2:
        return blocks
    ahead = ring_walk(members)
    left, right = blocks[-2][1][0], blocks[-1][1][0]
    if earlier:
        left, right = after((left, right), *earlier)
    cut_at = left.shape[0] // 2
    first = lax.ppermute(left[:cut_at], "chan", ahead)
    second = lax.ppermute(right[cut_at:], "chan", [(b, a) for a, b in ahead])
    return blocks + [(members // 2, [first, second])]


def neighbours(blocks):
    return [array for step, arrays in blocks if step for array in arrays]


def chunk_starts(share):
    total, starts, seen = sum(CHUNK_WEIGHTS), [0], 0
    for weight in CHUNK_WEIGHTS:
        seen += weight
        starts.append(round(share * seen / total))
    return starts


def local(dests, members, raw, offsets, quality):
    windows = raw.shape[0]
    pair = 16 // (2 * windows)
    bins = F // dests
    share = bins // pair
    chips = dests // 2
    assert chips & (chips - 1) == 0
    starts = chunk_starts(share)
    chunks = list(zip(starts[:-1], starts[1:]))
    table = jnp.asarray(dft_table())

    keep, give = spectra(raw, offsets, quality, table, dests)
    other = lax.ppermute(give, "win", [(i, i ^ 1) for i in range(dests)])
    own = join([(keep, 0, 0, 1), (other, 0, 0, 1)], share)
    own_start = ring_start(own, members)
    own_blocks = ring_finish(own_start, members)

    pieces = []
    for start, stop in chunks:
        came = []
        for k in range(1, chips):
            sent = join([(keep, start, k, 1), (other, start, k, 1)], stop - start)
            if pieces:
                sent = after([sent], *neighbours(own_start), pieces[-1][0])[0]
            came.append(lax.ppermute(sent, "win", [(i, i ^ (2 * k)) for i in range(dests)]))
        pieces.append(came)

    out = None
    for n, ((start, stop), came) in enumerate(zip(chunks, pieces)):
        far = join([(x, 0, 0, 2) for x in came], stop - start)
        begun = ring_start(far, members)
        blocks = ring_finish(begun, members, *([] if out is None else [out]))
        steps = []
        for (step, own_arrays), (_, arrays) in zip(own_blocks, blocks):
            views = [(x, 0, (0, x.shape[0])) for x in own_arrays] + [(x, start, (0, x.shape[0])) for x in arrays]
            steps.append((step, views))
        left = turn(steps[0][1], start, stop - start, windows)
        out = stack(left, start, steps, out, start, stop - start, bins, dests * windows)
    return out


def solution(mesh):
    in_specs = (P("win", None, "chan"), P("win"), P("win", "chan"))
    out_specs = P("win", None, "chan", None)
    run = functools.partial(local, mesh.shape["win"], mesh.shape["chan"])
    return jax.shard_map(run, mesh=mesh, in_specs=in_specs, out_specs=out_specs, check_vma=False)
```

```python
import functools
import math

import jax
import jax.numpy as jnp
import ml_dtypes
import numpy as np
from jax import lax
from jax.experimental import pallas as pl
from jax.experimental.pallas import tpu as pltpu
from jax.sharding import PartitionSpec as P

F = 384
L = 3072
FIRST_BIN = 60
CHUNK_WEIGHTS = (1, 1, 1)
STEP_GROUPS = 2
SPECTRA_MIB = 50

epsilon = 1e-05
MIB = 1024 * 1024


def dft_table():
    sample_idx = np.arange(L, dtype=np.int64)
    bin_idx = FIRST_BIN + np.arange(F, dtype=np.int64)
    residue = bin_idx[:, None] * sample_idx[None, :] % L
    angles = residue.astype(np.float32) * np.float32(2.0 * math.pi / L)
    return np.concatenate([np.cos(angles), -np.sin(angles)], 0).astype(ml_dtypes.bfloat16)


def interleave(windows, bins):
    pair = 16 // (2 * windows)
    rows = 2 * windows * bins
    row = lax.broadcasted_iota(jnp.int32, (rows, rows), 0)
    col = lax.broadcasted_iota(jnp.int32, (rows, rows), 1)
    w, p = row & (windows - 1), (row >> 3) & 1
    b, g = (row & 7) >> (windows.bit_length() - 1), row >> 4
    return jnp.where(col == (w * 2 + p) * bins + g * pair + b, 1.0, 0.0).astype(jnp.bfloat16)


def cut(raw_ref, slot, shift_at, window_ref):
    width = raw_ref.shape[2]
    spare = raw_ref.shape[1] - L
    tile = 256
    base = jnp.minimum(shift_at // 16, (spare - 16) // 16) * 16
    rest = shift_at - base
    whole = rest // 8
    fine = rest - whole * 8
    back = jnp.where(fine == 0, 0, 8 - fine)
    keep = lax.broadcasted_iota(jnp.int32, (tile // 8, 8, width), 1) < 8 - fine
    count = tile // 8
    for step in range(L // tile):
        start = pl.multiple_of(base + step * tile, 16)
        rows = raw_ref[slot, pl.ds(start, tile + 16), :].astype(jnp.float32).reshape(count + 2, 8, width)
        rolled = pltpu.roll(rows, back, 1)
        upper = jnp.where(whole == 0, rolled[1 : count + 1], rolled[2:])
        lower = jnp.where(whole == 0, rolled[:count], jnp.where(whole == 1, rolled[1 : count + 1], rolled[2:]))
        moved = jnp.where(keep, lower, upper)
        window_ref[step * tile : (step + 1) * tile, :] = moved.reshape(tile, width).astype(jnp.bfloat16)


def spectra_kernel(offsets_ref, table_hbm, raw_hbm, quality_hbm, keep_ref, give_ref, *scratch):
    table_ref, quality_ref, raw_ref, white, mixed, sems = scratch[:6]
    cuts = scratch[6:]
    windows, _, width = raw_ref.shape
    loads = [pltpu.make_async_copy(raw_hbm.at[w], raw_ref.at[w], sems.at[w]) for w in range(windows)]
    table_load = pltpu.make_async_copy(table_hbm, table_ref, sems.at[windows])
    quality_load = pltpu.make_async_copy(quality_hbm, quality_ref, sems.at[windows + 1])
    early = min(2, windows)
    for load in (*loads[:early], table_load, *loads[early:], quality_load):
        load.start()
    mix = interleave(windows, 256 // (2 * windows))
    for w in range(early):
        loads[w].wait()
        cut(raw_ref, w, offsets_ref[w], cuts[w])
    for load in (table_load, *loads[early:], quality_load):
        load.wait()
    for w in range(windows):
        if w + early < windows:
            cut(raw_ref, w + early, offsets_ref[w + early], cuts[w + early])
        transform = jnp.dot(table_ref[...], cuts[w][...], preferred_element_type=jnp.float32)
        band_power = jnp.sum(transform * transform, axis=0, keepdims=True) / F
        usable = quality_ref[w : w + 1, :].astype(jnp.float32)
        white[w] = (transform * (lax.rsqrt(band_power + epsilon) * usable)).astype(jnp.bfloat16)

    pair = 16 // (2 * windows)
    bins = mix.shape[0] // (2 * windows)
    groups = bins // pair
    for block in range(F // bins):
        parts = [
            white[v, p * F + block * bins : p * F + (block + 1) * bins, :] for v in range(windows) for p in range(2)
        ]
        product = jnp.dot(mix, jnp.concatenate(parts, 0), preferred_element_type=jnp.float32)
        mixed[block * groups : (block + 1) * groups] = product.astype(jnp.bfloat16).reshape(groups, 16, width)
    me = lax.axis_index("win")
    chip, core = me // 2, me % 2
    chips, share = keep_ref.shape[:2]
    for k in range(chips):
        at = (chip ^ k) * 2 * share
        keep_ref[k] = mixed[pl.ds(at + core * share, share)]
        give_ref[k] = mixed[pl.ds(at + (1 - core) * share, share)]


def in_vmem(count):
    return [pl.BlockSpec(memory_space=pltpu.VMEM)] * count


def spectra(raw, offsets, quality, table, dests):
    windows, _, width = raw.shape
    groups = F * 2 * windows // 16
    blocks = (dests // 2, groups // dests, 16, width)
    return pl.pallas_call(
        spectra_kernel,
        in_specs=[pl.BlockSpec(memory_space=pltpu.SMEM)] + [pl.BlockSpec(memory_space=pl.ANY)] * 3,
        out_specs=in_vmem(2),
        scratch_shapes=[
            pltpu.VMEM(table.shape, table.dtype),
            pltpu.VMEM(quality.shape, quality.dtype),
            pltpu.VMEM(raw.shape, raw.dtype),
            pltpu.VMEM((windows, 2 * F, width), jnp.bfloat16),
            pltpu.VMEM((groups, 16, width), jnp.bfloat16),
            pltpu.SemaphoreType.DMA((windows + 2,)),
            *[pltpu.VMEM((L, width), jnp.bfloat16)] * windows,
        ],
        out_shape=[jax.ShapeDtypeStruct(blocks, jnp.bfloat16)] * 2,
        compiler_params=pltpu.CompilerParams(vmem_limit_bytes=SPECTRA_MIB * MIB),
        cost_estimate=pl.CostEstimate(
            flops=2 * windows * 2 * F * L * width, bytes_accessed=2 * windows * raw.shape[1] * width + 4 * F * L, transcendentals=0
        ),
        name="spectra",
    )(offsets, table, raw, quality)


def join_kernel(moves, *refs):
    out_ref = refs[-1]
    groups = out_ref.shape[1]
    to = 0
    for i, at, source, count in moves:
        out_ref[to : to + count] = refs[i][source : source + count, at : at + groups]
        to += count


def join(views, groups):
    arrays, moves = [], []
    for x, *where in views:
        known = [i for i, y in enumerate(arrays) if y is x]
        if not known:
            arrays.append(x)
        moves.append((known[0] if known else len(arrays) - 1, *where))
    shape = (sum(move[3] for move in moves), groups, *arrays[0].shape[2:])
    return pl.pallas_call(
        functools.partial(join_kernel, moves),
        in_specs=in_vmem(len(arrays)),
        out_specs=in_vmem(1)[0],
        out_shape=jax.ShapeDtypeStruct(shape, arrays[0].dtype),
        compiler_params=pltpu.CompilerParams(vmem_limit_bytes=12 * MIB),
        cost_estimate=pl.CostEstimate(flops=0, bytes_accessed=4 * math.prod(shape), transcendentals=0),
        name="join",
    )(*arrays)


def view(ref, group, at, sources):
    return ref[sources[0] : sources[1], group - at].reshape(-1, ref.shape[-1])


def turn_kernel(windows, first_group, views, *refs):
    out_ref = refs[-1]
    _, pair, _, width, depth = out_ref.shape
    bin_of = lax.broadcasted_iota(jnp.int32, (width, depth), 1) % 8 // windows

    def body(g, carry):
        x = jnp.concatenate([view(refs[i], first_group + g, *where) for i, where in enumerate(views)], 0)
        by_part = x.astype(jnp.float32).reshape(depth // 16, 16, width)
        turned = jnp.concatenate([by_part[:, 8:], -by_part[:, :8]], 1)
        for part, rows in enumerate((by_part, turned)):
            left = rows.reshape(depth, width).T
            for b in range(pair):
                out_ref[g, b, part] = jnp.where(bin_of == b, left, 0.0).astype(jnp.bfloat16)
        return carry

    lax.fori_loop(0, out_ref.shape[0], body, 0)


def turn(items, first_group, groups, windows):
    rows, width = items[0][0].shape[2:]
    depth = sum(sources[1] - sources[0] for _, _, sources in items) * rows
    pair = 16 // (2 * windows)
    return pl.pallas_call(
        functools.partial(turn_kernel, windows, first_group, [item[1:] for item in items]),
        in_specs=in_vmem(len(items)),
        out_specs=in_vmem(1)[0],
        out_shape=jax.ShapeDtypeStruct((groups, pair, 2, width, depth), jnp.bfloat16),
        compiler_params=pltpu.CompilerParams(vmem_limit_bytes=12 * MIB),
        cost_estimate=pl.CostEstimate(flops=0, bytes_accessed=8 * groups * width * depth, transcendentals=0),
        name="turn",
    )(*[item[0] for item in items])


def closed_walk(i, members):
    return jnp.where(i < members // 2, i, members - 1 - i + members // 2)


def stack_kernel(scale, left_first, first_group, groups, step_groups, layout, left_ref, *refs):
    out_ref, tiles, sems = refs[-3:]
    pair, _, width, _ = left_ref.shape[1:]
    members = len(layout)
    where = closed_walk(lax.axis_index("chan"), members)
    columns = []
    for step, _ in layout:
        column = closed_walk(lax.rem(where + (step + members), members), members)
        columns.append(pl.ds(pl.multiple_of(column * width, width), width))

    def leave(slot, g, b, part):
        return pltpu.make_async_copy(tiles.at[slot], out_ref.at[g * pair + b, part], sems.at[slot])

    def body(i, carry):
        for s in range(step_groups):
            g = first_group + i * step_groups + s
            rights = [
                jnp.concatenate([view(refs[n], g, *item) for n, item in items], 0) for _, items in layout
            ]
            for b in range(pair):
                for part in range(2):
                    slot = (s * pair + b) * 2 + part

                    @pl.when(i > 0)
                    def _():
                        leave(slot, g - step_groups, b, part).wait()

                    left = left_ref[g - left_first, b, part]
                    for right, where_to in zip(rights, columns):
                        product = jnp.dot(left, right, preferred_element_type=jnp.float32)
                        tiles[slot, :, where_to] = (product * scale).astype(jnp.bfloat16)
                    leave(slot, g, b, part).start()
        return carry

    lax.fori_loop(0, groups // step_groups, body, 0)
    for s in range(step_groups):
        for b in range(pair):
            for part in range(2):
                leave((s * pair + b) * 2 + part, first_group + groups - step_groups + s, b, part).wait()


def stack(left, left_first, steps, into, first_group, groups, bins, sources):
    members = len(steps)
    _, pair, _, width, depth = left.shape
    step_groups = max(n for n in range(1, STEP_GROUPS + 1) if groups % n == 0)
    operands, layout = [left], []
    for step, items in steps:
        layout.append((step, [(len(operands) - 1 + i, item[1:]) for i, item in enumerate(items)]))
        operands += [item[0] for item in items]
    in_specs = in_vmem(len(operands))
    aliases = {}
    if into is not None:
        aliases = {len(operands): 0}
        operands.append(into)
        in_specs.append(pl.BlockSpec(memory_space=pl.ANY))
    slots = step_groups * pair * 2
    return pl.pallas_call(
        functools.partial(
            stack_kernel, 1.0 / math.sqrt(sources), left_first, first_group, groups, step_groups, layout
        ),
        in_specs=in_specs,
        out_specs=pl.BlockSpec(memory_space=pl.ANY),
        out_shape=jax.ShapeDtypeStruct((bins, 2, width, members * width), jnp.bfloat16),
        scratch_shapes=[
            pltpu.VMEM((slots, width, members * width), jnp.bfloat16),
            pltpu.SemaphoreType.DMA((slots,)),
        ],
        input_output_aliases=aliases,
        compiler_params=pltpu.CompilerParams(vmem_limit_bytes=24 * MIB),
        cost_estimate=pl.CostEstimate(
            flops=4 * groups * pair * depth * width * width * members,
            bytes_accessed=4 * groups * pair * width * members * width,
            transcendentals=0,
        ),
        name="stack",
    )(*operands)


def after(arrays, *earlier):
    return list(lax.optimization_barrier((tuple(arrays), earlier))[0])


def ring_walk(members):
    ring = [i if i < members // 2 else members - 1 - i + members // 2 for i in range(members)]
    return [(ring[i], ring[(i + 1) % members]) for i in range(members)]


def ring_start(x, members):
    ahead = ring_walk(members)
    back = [(b, a) for a, b in ahead]
    left = right = x
    blocks = [(0, [x])]
    for step in range(1, (members + 1) // 2):
        left = lax.ppermute(left, "chan", ahead)
        right = lax.ppermute(right, "chan", back)
        blocks += [(-step, [left]), (step, [right])]
    return blocks


def ring_finish(blocks, members, *earlier):
    if members % 2:
        return blocks
    ahead = ring_walk(members)
    left, right = blocks[-2][1][0], blocks[-1][1][0]
    if earlier:
        left, right = after((left, right), *earlier)
    cut_at = left.shape[0] // 2
    first = lax.ppermute(left[:cut_at], "chan", ahead)
    second = lax.ppermute(right[cut_at:], "chan", [(b, a) for a, b in ahead])
    return blocks + [(members // 2, [first, second])]


def neighbours(blocks):
    return [array for step, arrays in blocks if step for array in arrays]


def chunk_starts(share):
    total, starts, seen = sum(CHUNK_WEIGHTS), [0], 0
    for weight in CHUNK_WEIGHTS:
        seen += weight
        starts.append(round(share * seen / total))
    return starts


def local(dests, members, raw, offsets, quality):
    windows = raw.shape[0]
    pair = 16 // (2 * windows)
    bins = F // dests
    share = bins // pair
    chips = dests // 2
    assert chips & (chips - 1) == 0
    starts = chunk_starts(share)
    chunks = list(zip(starts[:-1], starts[1:]))
    table = jnp.asarray(dft_table())

    keep, give = spectra(raw, offsets, quality, table, dests)
    other = lax.ppermute(give, "win", [(i, i ^ 1) for i in range(dests)])
    own = join([(keep, 0, 0, 1), (other, 0, 0, 1)], share)
    own_start = ring_start(own, members)
    own_blocks = ring_finish(own_start, members)

    pieces = []
    for start, stop in chunks:
        came = []
        for k in range(1, chips):
            sent = join([(keep, start, k, 1), (other, start, k, 1)], stop - start)
            if pieces:
                sent = after([sent], *neighbours(own_start), pieces[-1][0])[0]
            came.append(lax.ppermute(sent, "win", [(i, i ^ (2 * k)) for i in range(dests)]))
        pieces.append(came)

    out = None
    for n, ((start, stop), came) in enumerate(zip(chunks, pieces)):
        far = join([(x, 0, 0, 2) for x in came], stop - start)
        begun = ring_start(far, members)
        blocks = ring_finish(begun, members, *([] if out is None else [out]))
        steps = []
        for (step, own_arrays), (_, arrays) in zip(own_blocks, blocks):
            views = [(x, 0, (0, x.shape[0])) for x in own_arrays] + [(x, start, (0, x.shape[0])) for x in arrays]
            steps.append((step, views))
        left = turn(steps[0][1], start, stop - start, windows)
        out = stack(left, start, steps, out, start, stop - start, bins, dests * windows)
    return out


def solution(mesh):
    in_specs = (P("win", None, "chan"), P("win"), P("win", "chan"))
    out_specs = P("win", None, "chan", None)
    run = functools.partial(local, mesh.shape["win"], mesh.shape["chan"])
    return jax.shard_map(run, mesh=mesh, in_specs=in_specs, out_specs=out_specs, check_vma=False)
```

```python
import functools
import math

import jax
import jax.numpy as jnp
import ml_dtypes
import numpy as np
from jax import lax
from jax.experimental import pallas as pl
from jax.experimental.pallas import tpu as pltpu
from jax.sharding import PartitionSpec as P

F = 384
L = 3072
FIRST_BIN = 60
CHUNK_WEIGHTS = (1, 1, 1)
STEP_GROUPS = 2
SPECTRA_MIB = 50

epsilon = 1e-05
MIB = 1024 * 1024


def dft_table():
    sample_idx = np.arange(L, dtype=np.int64)
    bin_idx = FIRST_BIN + np.arange(F, dtype=np.int64)
    residue = bin_idx[:, None] * sample_idx[None, :] % L
    angles = residue.astype(np.float32) * np.float32(2.0 * math.pi / L)
    return np.concatenate([np.cos(angles), -np.sin(angles)], 0).astype(ml_dtypes.bfloat16)


def interleave(windows, bins):
    pair = 16 // (2 * windows)
    rows = 2 * windows * bins
    row = lax.broadcasted_iota(jnp.int32, (rows, rows), 0)
    col = lax.broadcasted_iota(jnp.int32, (rows, rows), 1)
    w, p = row & (windows - 1), (row >> 3) & 1
    b, g = (row & 7) >> (windows.bit_length() - 1), row >> 4
    return jnp.where(col == (w * 2 + p) * bins + g * pair + b, 1.0, 0.0).astype(jnp.bfloat16)


def cut(raw_ref, slot, shift_at, window_ref):
    width = raw_ref.shape[2]
    spare = raw_ref.shape[1] - L
    tile = 256
    base = jnp.minimum(shift_at // 16, (spare - 16) // 16) * 16
    rest = shift_at - base
    whole = rest // 8
    fine = rest - whole * 8
    back = jnp.where(fine == 0, 0, 8 - fine)
    keep = lax.broadcasted_iota(jnp.int32, (tile // 8, 8, width), 1) < 8 - fine
    count = tile // 8
    for step in range(L // tile):
        start = pl.multiple_of(base + step * tile, 16)
        rows = raw_ref[slot, pl.ds(start, tile + 16), :].astype(jnp.float32).reshape(count + 2, 8, width)
        rolled = pltpu.roll(rows, back, 1)
        upper = jnp.where(whole == 0, rolled[1 : count + 1], rolled[2:])
        lower = jnp.where(whole == 0, rolled[:count], jnp.where(whole == 1, rolled[1 : count + 1], rolled[2:]))
        moved = jnp.where(keep, lower, upper)
        window_ref[step * tile : (step + 1) * tile, :] = moved.reshape(tile, width).astype(jnp.bfloat16)


def spectra_kernel(chips, offsets_ref, table_hbm, raw_hbm, quality_hbm, keep_ref, give_ref, *scratch):
    table_ref, quality_ref, raw_ref, white, mixed, sems = scratch[:6]
    cuts = scratch[6:]
    windows, _, width = raw_ref.shape
    loads = [pltpu.make_async_copy(raw_hbm.at[w], raw_ref.at[w], sems.at[w]) for w in range(windows)]
    table_load = pltpu.make_async_copy(table_hbm, table_ref, sems.at[windows])
    quality_load = pltpu.make_async_copy(quality_hbm, quality_ref, sems.at[windows + 1])
    early = min(2, windows)
    for load in (*loads[:early], table_load, *loads[early:], quality_load):
        load.start()
    mix = interleave(windows, 256 // (2 * windows))
    for w in range(early):
        loads[w].wait()
        cut(raw_ref, w, offsets_ref[w], cuts[w])
    for load in (table_load, *loads[early:], quality_load):
        load.wait()
    for w in range(windows):
        if w + early < windows:
            cut(raw_ref, w + early, offsets_ref[w + early], cuts[w + early])
        transform = jnp.dot(table_ref[...], cuts[w][...], preferred_element_type=jnp.float32)
        band_power = jnp.sum(transform * transform, axis=0, keepdims=True) / F
        usable = quality_ref[w : w + 1, :].astype(jnp.float32)
        white[w] = (transform * (lax.rsqrt(band_power + epsilon) * usable)).astype(jnp.bfloat16)

    pair = 16 // (2 * windows)
    bins = mix.shape[0] // (2 * windows)
    groups = bins // pair
    for block in range(F // bins):
        parts = [
            white[v, p * F + block * bins : p * F + (block + 1) * bins, :] for v in range(windows) for p in range(2)
        ]
        product = jnp.dot(mix, jnp.concatenate(parts, 0), preferred_element_type=jnp.float32)
        mixed[block * groups : (block + 1) * groups] = product.astype(jnp.bfloat16).reshape(groups, 16, width)
    me = lax.axis_index("win")
    chip, core = me // 2, me % 2
    share = keep_ref.shape[0] // chips
    for k in range(chips):
        at = (chip ^ k) * 2 * share
        keep_ref[k * share : (k + 1) * share] = mixed[pl.ds(at + core * share, share)]
        give_ref[k * share : (k + 1) * share] = mixed[pl.ds(at + (1 - core) * share, share)]


def in_vmem(count):
    return [pl.BlockSpec(memory_space=pltpu.VMEM)] * count


def spectra(raw, offsets, quality, table, dests):
    windows, _, width = raw.shape
    groups = F * 2 * windows // 16
    blocks = (groups // 2, 16, width)
    return pl.pallas_call(
        functools.partial(spectra_kernel, dests // 2),
        in_specs=[pl.BlockSpec(memory_space=pltpu.SMEM)] + [pl.BlockSpec(memory_space=pl.ANY)] * 3,
        out_specs=in_vmem(2),
        scratch_shapes=[
            pltpu.VMEM(table.shape, table.dtype),
            pltpu.VMEM(quality.shape, quality.dtype),
            pltpu.VMEM(raw.shape, raw.dtype),
            pltpu.VMEM((windows, 2 * F, width), jnp.bfloat16),
            pltpu.VMEM((groups, 16, width), jnp.bfloat16),
            pltpu.SemaphoreType.DMA((windows + 2,)),
            *[pltpu.VMEM((L, width), jnp.bfloat16)] * windows,
        ],
        out_shape=[jax.ShapeDtypeStruct(blocks, jnp.bfloat16)] * 2,
        compiler_params=pltpu.CompilerParams(vmem_limit_bytes=SPECTRA_MIB * MIB),
        cost_estimate=pl.CostEstimate(
            flops=2 * windows * 2 * F * L * width, bytes_accessed=2 * windows * raw.shape[1] * width + 4 * F * L, transcendentals=0
        ),
        name="spectra",
    )(offsets, table, raw, quality)


def part_of(view, low, high):
    x, base, _, groups, first = view
    return (x, base + low * groups, high - low, groups, first)


def join_kernel(moves, *refs):
    out_ref = refs[-1]
    to = 0
    for i, at, count in moves:
        out_ref[to : to + count] = refs[i][at : at + count]
        to += count


def join(views):
    arrays, moves, places, to = [], [], [], 0
    for x, base, sources, groups, first in views:
        known = [i for i, y in enumerate(arrays) if y is x]
        if not known:
            arrays.append(x)
        moves.append((known[0] if known else len(arrays) - 1, base, sources * groups))
        places.append((to, sources, groups, first))
        to += sources * groups
    shape = (to, *arrays[0].shape[1:])
    joined = pl.pallas_call(
        functools.partial(join_kernel, moves),
        in_specs=in_vmem(len(arrays)),
        out_specs=in_vmem(1)[0],
        out_shape=jax.ShapeDtypeStruct(shape, arrays[0].dtype),
        compiler_params=pltpu.CompilerParams(vmem_limit_bytes=12 * MIB),
        cost_estimate=pl.CostEstimate(flops=0, bytes_accessed=4 * math.prod(shape), transcendentals=0),
        name="join",
    )(*arrays)
    return joined, places


def gathered(ref, group, place):
    base, sources, groups, first = place
    return [ref[base + source * groups + group - first] for source in range(sources)]


def operands_of(views):
    arrays, places = [], []
    for x, *place in views:
        known = [i for i, y in enumerate(arrays) if y is x]
        if not known:
            arrays.append(x)
        places.append((known[0] if known else len(arrays) - 1, place))
    return arrays, places


def turn_kernel(windows, first_group, views, *refs):
    out_ref = refs[-1]
    _, pair, _, width, depth = out_ref.shape
    bin_of = lax.broadcasted_iota(jnp.int32, (width, depth), 1) % 8 // windows

    def body(g, carry):
        x = jnp.concatenate(sum([gathered(refs[i], first_group + g, place) for i, place in views], []), 0)
        by_part = x.astype(jnp.float32).reshape(depth // 16, 16, width)
        turned = jnp.concatenate([by_part[:, 8:], -by_part[:, :8]], 1)
        for part, rows in enumerate((by_part, turned)):
            left = rows.reshape(depth, width).T
            for b in range(pair):
                out_ref[g, b, part] = jnp.where(bin_of == b, left, 0.0).astype(jnp.bfloat16)
        return carry

    lax.fori_loop(0, out_ref.shape[0], body, 0)


def turn(views, first_group, groups, windows):
    arrays, places = operands_of(views)
    rows, width = arrays[0].shape[1:]
    depth = sum(place[1] for _, place in places) * rows
    pair = 16 // (2 * windows)
    return pl.pallas_call(
        functools.partial(turn_kernel, windows, first_group, places),
        in_specs=in_vmem(len(arrays)),
        out_specs=in_vmem(1)[0],
        out_shape=jax.ShapeDtypeStruct((groups, pair, 2, width, depth), jnp.bfloat16),
        compiler_params=pltpu.CompilerParams(vmem_limit_bytes=12 * MIB),
        cost_estimate=pl.CostEstimate(flops=0, bytes_accessed=8 * groups * width * depth, transcendentals=0),
        name="turn",
    )(*arrays)


def closed_walk(i, members):
    return jnp.where(i < members // 2, i, members - 1 - i + members // 2)


def stack_kernel(scale, left_first, first_group, layout, left_ref, *refs):
    out_ref = refs[-1]
    pair, _, width, _ = left_ref.shape[1:]
    step_groups = out_ref.shape[0] // pair
    members = len(layout)
    where = closed_walk(lax.axis_index("chan"), members)
    for s in range(step_groups):
        g = pl.program_id(0) * step_groups + s
        for step, items in layout:
            right = jnp.concatenate(sum([gathered(refs[i], first_group + g, place) for i, place in items], []), 0)
            column = closed_walk(lax.rem(where + (step + members), members), members)
            columns = pl.ds(pl.multiple_of(column * width, width), width)
            for b in range(pair):
                for part in range(2):
                    left = left_ref[first_group - left_first + g, b, part]
                    product = jnp.dot(left, right, preferred_element_type=jnp.float32)
                    out_ref[s * pair + b, part, :, columns] = (product * scale).astype(jnp.bfloat16)


def stack(left, left_first, steps, into, first_group, groups, bins, sources):
    members = len(steps)
    _, pair, _, width, depth = left.shape
    step_groups = max(n for n in range(1, STEP_GROUPS + 1) if groups % n == 0 and first_group % n == 0)
    arrays, places = operands_of(sum([views for _, views in steps], []))
    layout = []
    for step, views in steps:
        layout.append((step, places[: len(views)]))
        places = places[len(views) :]
    operands = [left, *arrays]
    in_specs = in_vmem(len(operands))
    aliases = {}
    if into is not None:
        aliases = {len(operands): 0}
        operands.append(into)
        in_specs.append(pl.BlockSpec(memory_space=pl.ANY))
    block = (step_groups * pair, 2, width, members * width)
    return pl.pallas_call(
        functools.partial(stack_kernel, 1.0 / math.sqrt(sources), left_first, first_group, layout),
        grid=(groups // step_groups,),
        in_specs=in_specs,
        out_specs=pl.BlockSpec(block, lambda g: (first_group // step_groups + g, 0, 0, 0)),
        out_shape=jax.ShapeDtypeStruct((bins, 2, width, members * width), jnp.bfloat16),
        input_output_aliases=aliases,
        compiler_params=pltpu.CompilerParams(vmem_limit_bytes=24 * MIB, dimension_semantics=("arbitrary",)),
        cost_estimate=pl.CostEstimate(
            flops=4 * groups * pair * depth * width * width * members,
            bytes_accessed=4 * groups * pair * width * members * width,
            transcendentals=0,
        ),
        name="stack",
    )(*operands)


def after(arrays, *earlier):
    return list(lax.optimization_barrier((tuple(arrays), earlier))[0])


def ring_walk(members):
    ring = [i if i < members // 2 else members - 1 - i + members // 2 for i in range(members)]
    return [(ring[i], ring[(i + 1) % members]) for i in range(members)]


def halves_of(views, total):
    first, second, seen = [], [], 0
    for view in views:
        cut_at = min(max(total // 2 - seen, 0), view[2])
        first += [part_of(view, 0, cut_at)] if cut_at else []
        second += [part_of(view, cut_at, view[2])] if cut_at < view[2] else []
        seen += view[2]
    return first, second


def ring_phase(travellers, members):
    ahead = ring_walk(members)
    moved = []
    for way, pairs in ((0, ahead), (1, [(b, a) for a, b in ahead])):
        sent, places = join(sum([views[way] for views in travellers], []))
        came = lax.ppermute(sent, "chan", pairs)
        moved.append([(came, *place) for place in places])
    result = []
    for views in travellers:
        result.append((moved[0][: len(views[0])], moved[1][: len(views[1])]))
        moved = [moved[0][len(views[0]) :], moved[1][len(views[1]) :]]
    return result


def chunk_starts(share):
    total, starts, seen = sum(CHUNK_WEIGHTS), [0], 0
    for weight in CHUNK_WEIGHTS:
        seen += weight
        starts.append(round(share * seen / total))
    return starts


def local(dests, members, raw, offsets, quality):
    windows = raw.shape[0]
    pair = 16 // (2 * windows)
    bins = F // dests
    share = bins // pair
    chips = dests // 2
    assert chips & (chips - 1) == 0
    starts = chunk_starts(share)
    chunks = list(zip(starts[:-1], starts[1:]))
    table = jnp.asarray(dft_table())

    keep, give = spectra(raw, offsets, quality, table, dests)
    other = lax.ppermute(give, "win", [(i, i ^ 1) for i in range(dests)])
    def travel(n, *earlier):
        start, stop = chunks[n]
        came = []
        for k in range(1, chips):
            sent, _ = join([(x, k * share + start, 1, stop - start, start) for x in (keep, other)])
            if earlier:
                sent = after([sent], *earlier)[0]
            came.append(lax.ppermute(sent, "win", [(i, i ^ (2 * k)) for i in range(dests)]))
        return [(x, 0, 2, stop - start, start) for x in came]

    units = [[(x, 0, 1, share, 0) for x in (keep, other)]]
    turns = members // 2
    found = [[(0, units[0])]]
    held = [(units[0], units[0])]
    out = None
    stacked = 0
    for phase in range(len(chunks) + turns):
        travellers, who = [], []
        for u in range(len(units)):
            step = phase - u + 1
            if not 1 <= step <= turns:
                continue
            left, right = held[u]
            if step == turns:
                total = sum(view[2] for view in left)
                left, right = halves_of(left, total)[0], halves_of(right, total)[1]
            travellers.append((left, right))
            who.append((u, step))
        if phase < len(chunks):
            arrives = travel(phase, *([x[0] for x in units[-1][:1]] if phase else []))
        for (u, step), (left, right) in zip(who, ring_phase(travellers, members)):
            held[u] = (left, right)
            if step == turns:
                found[u].append((turns, left + right))
            else:
                found[u] += [(-step, left), (step, right)]
        if phase < len(chunks):
            units.append(arrives)
            held.append((arrives, arrives))
            found.append([(0, arrives)])
        while stacked < phase - turns or (phase + 1 == len(chunks) + turns and stacked < len(chunks)):
            start, stop = chunks[stacked]
            steps = [(a[0], a[1] + b[1]) for a, b in zip(found[0], found[stacked + 1])]
            left = turn(steps[0][1], start, stop - start, windows)
            out = stack(left, start, steps, out, start, stop - start, bins, dests * windows)
            stacked += 1
    return out


def solution(mesh):
    in_specs = (P("win", None, "chan"), P("win"), P("win", "chan"))
    out_specs = P("win", None, "chan", None)
    run = functools.partial(local, mesh.shape["win"], mesh.shape["chan"])
    return jax.shard_map(run, mesh=mesh, in_specs=in_specs, out_specs=out_specs, check_vma=False)
```

```python
import functools
import math

import jax
import jax.numpy as jnp
import ml_dtypes
import numpy as np
from jax import lax
from jax.experimental import pallas as pl
from jax.experimental.pallas import tpu as pltpu
from jax.sharding import PartitionSpec as P

F = 384
L = 3072
FIRST_BIN = 60
CHUNK_WEIGHTS = (1, 1, 1)
STEP_GROUPS = 2
SPECTRA_MIB = 50

epsilon = 1e-05
MIB = 1024 * 1024


def dft_table():
    sample_idx = np.arange(L, dtype=np.int64)
    bin_idx = FIRST_BIN + np.arange(F, dtype=np.int64)
    residue = bin_idx[:, None] * sample_idx[None, :] % L
    angles = residue.astype(np.float32) * np.float32(2.0 * math.pi / L)
    return np.concatenate([np.cos(angles), -np.sin(angles)], 0).astype(ml_dtypes.bfloat16)


def interleave(windows, bins):
    pair = 16 // (2 * windows)
    rows = 2 * windows * bins
    row = lax.broadcasted_iota(jnp.int32, (rows, rows), 0)
    col = lax.broadcasted_iota(jnp.int32, (rows, rows), 1)
    w, p = row & (windows - 1), (row >> 3) & 1
    b, g = (row & 7) >> (windows.bit_length() - 1), row >> 4
    return jnp.where(col == (w * 2 + p) * bins + g * pair + b, 1.0, 0.0).astype(jnp.bfloat16)


def cut(raw_ref, slot, shift_at, window_ref):
    width = raw_ref.shape[2]
    spare = raw_ref.shape[1] - L
    tile = 256
    base = jnp.minimum(shift_at // 16, (spare - 16) // 16) * 16
    rest = shift_at - base
    whole = rest // 8
    fine = rest - whole * 8
    back = jnp.where(fine == 0, 0, 8 - fine)
    keep = lax.broadcasted_iota(jnp.int32, (tile // 8, 8, width), 1) < 8 - fine
    count = tile // 8
    for step in range(L // tile):
        start = pl.multiple_of(base + step * tile, 16)
        rows = raw_ref[slot, pl.ds(start, tile + 16), :].astype(jnp.float32).reshape(count + 2, 8, width)
        rolled = pltpu.roll(rows, back, 1)
        upper = jnp.where(whole == 0, rolled[1 : count + 1], rolled[2:])
        lower = jnp.where(whole == 0, rolled[:count], jnp.where(whole == 1, rolled[1 : count + 1], rolled[2:]))
        moved = jnp.where(keep, lower, upper)
        window_ref[step * tile : (step + 1) * tile, :] = moved.reshape(tile, width).astype(jnp.bfloat16)


def spectra_kernel(chips, offsets_ref, table_hbm, raw_hbm, quality_hbm, keep_ref, give_ref, *scratch):
    table_ref, quality_ref, raw_ref, white, mixed, sems = scratch[:6]
    cuts = scratch[6:]
    windows, _, width = raw_ref.shape
    loads = [pltpu.make_async_copy(raw_hbm.at[w], raw_ref.at[w], sems.at[w]) for w in range(windows)]
    table_load = pltpu.make_async_copy(table_hbm, table_ref, sems.at[windows])
    quality_load = pltpu.make_async_copy(quality_hbm, quality_ref, sems.at[windows + 1])
    early = min(2, windows)
    for load in (*loads[:early], table_load, *loads[early:], quality_load):
        load.start()
    mix = interleave(windows, 256 // (2 * windows))
    for w in range(early):
        loads[w].wait()
        cut(raw_ref, w, offsets_ref[w], cuts[w])
    for load in (table_load, *loads[early:], quality_load):
        load.wait()
    for w in range(windows):
        if w + early < windows:
            cut(raw_ref, w + early, offsets_ref[w + early], cuts[w + early])
        transform = jnp.dot(table_ref[...], cuts[w][...], preferred_element_type=jnp.float32)
        band_power = jnp.sum(transform * transform, axis=0, keepdims=True) / F
        usable = quality_ref[w : w + 1, :].astype(jnp.float32)
        white[w] = (transform * (lax.rsqrt(band_power + epsilon) * usable)).astype(jnp.bfloat16)

    pair = 16 // (2 * windows)
    bins = mix.shape[0] // (2 * windows)
    groups = bins // pair
    for block in range(F // bins):
        parts = [
            white[v, p * F + block * bins : p * F + (block + 1) * bins, :] for v in range(windows) for p in range(2)
        ]
        product = jnp.dot(mix, jnp.concatenate(parts, 0), preferred_element_type=jnp.float32)
        mixed[block * groups : (block + 1) * groups] = product.astype(jnp.bfloat16).reshape(groups, 16, width)
    me = lax.axis_index("win")
    chip, core = me // 2, me % 2
    share = keep_ref.shape[0] // chips
    for k in range(chips):
        at = (chip ^ k) * 2 * share
        keep_ref[k * share : (k + 1) * share] = mixed[pl.ds(at + core * share, share)]
        give_ref[k * share : (k + 1) * share] = mixed[pl.ds(at + (1 - core) * share, share)]


def in_vmem(count):
    return [pl.BlockSpec(memory_space=pltpu.VMEM)] * count


def spectra(raw, offsets, quality, table, dests):
    windows, _, width = raw.shape
    groups = F * 2 * windows // 16
    blocks = (groups // 2, 16, width)
    return pl.pallas_call(
        functools.partial(spectra_kernel, dests // 2),
        in_specs=[pl.BlockSpec(memory_space=pltpu.SMEM)] + [pl.BlockSpec(memory_space=pl.ANY)] * 3,
        out_specs=in_vmem(2),
        scratch_shapes=[
            pltpu.VMEM(table.shape, table.dtype),
            pltpu.VMEM(quality.shape, quality.dtype),
            pltpu.VMEM(raw.shape, raw.dtype),
            pltpu.VMEM((windows, 2 * F, width), jnp.bfloat16),
            pltpu.VMEM((groups, 16, width), jnp.bfloat16),
            pltpu.SemaphoreType.DMA((windows + 2,)),
            *[pltpu.VMEM((L, width), jnp.bfloat16)] * windows,
        ],
        out_shape=[jax.ShapeDtypeStruct(blocks, jnp.bfloat16)] * 2,
        compiler_params=pltpu.CompilerParams(vmem_limit_bytes=SPECTRA_MIB * MIB),
        cost_estimate=pl.CostEstimate(
            flops=2 * windows * 2 * F * L * width, bytes_accessed=2 * windows * raw.shape[1] * width + 4 * F * L, transcendentals=0
        ),
        name="spectra",
    )(offsets, table, raw, quality)


def part_of(view, low, high):
    x, base, _, groups, first = view
    return (x, base + low * groups, high - low, groups, first)


def join_kernel(moves, *refs):
    out_ref = refs[-1]
    to = 0
    for i, at, count in moves:
        out_ref[to : to + count] = refs[i][at : at + count]
        to += count


def join(views):
    arrays, moves, places, to = [], [], [], 0
    for x, base, sources, groups, first in views:
        known = [i for i, y in enumerate(arrays) if y is x]
        if not known:
            arrays.append(x)
        moves.append((known[0] if known else len(arrays) - 1, base, sources * groups))
        places.append((to, sources, groups, first))
        to += sources * groups
    shape = (to, *arrays[0].shape[1:])
    joined = pl.pallas_call(
        functools.partial(join_kernel, moves),
        in_specs=in_vmem(len(arrays)),
        out_specs=in_vmem(1)[0],
        out_shape=jax.ShapeDtypeStruct(shape, arrays[0].dtype),
        compiler_params=pltpu.CompilerParams(vmem_limit_bytes=12 * MIB),
        cost_estimate=pl.CostEstimate(flops=0, bytes_accessed=4 * math.prod(shape), transcendentals=0),
        name="join",
    )(*arrays)
    return joined, places


def gathered(ref, group, place):
    base, sources, groups, first = place
    return [ref[base + source * groups + group - first] for source in range(sources)]


def operands_of(views):
    arrays, places = [], []
    for x, *place in views:
        known = [i for i, y in enumerate(arrays) if y is x]
        if not known:
            arrays.append(x)
        places.append((known[0] if known else len(arrays) - 1, place))
    return arrays, places


def turn_kernel(windows, first_group, views, *refs):
    out_ref = refs[-1]
    _, pair, _, width, depth = out_ref.shape
    bin_of = lax.broadcasted_iota(jnp.int32, (width, depth), 1) % 8 // windows

    def body(g, carry):
        x = jnp.concatenate(sum([gathered(refs[i], first_group + g, place) for i, place in views], []), 0)
        by_part = x.astype(jnp.float32).reshape(depth // 16, 16, width)
        turned = jnp.concatenate([by_part[:, 8:], -by_part[:, :8]], 1)
        for part, rows in enumerate((by_part, turned)):
            left = rows.reshape(depth, width).T
            for b in range(pair):
                out_ref[g, b, part] = jnp.where(bin_of == b, left, 0.0).astype(jnp.bfloat16)
        return carry

    lax.fori_loop(0, out_ref.shape[0], body, 0)


def turn(views, first_group, groups, windows):
    arrays, places = operands_of(views)
    rows, width = arrays[0].shape[1:]
    depth = sum(place[1] for _, place in places) * rows
    pair = 16 // (2 * windows)
    return pl.pallas_call(
        functools.partial(turn_kernel, windows, first_group, places),
        in_specs=in_vmem(len(arrays)),
        out_specs=in_vmem(1)[0],
        out_shape=jax.ShapeDtypeStruct((groups, pair, 2, width, depth), jnp.bfloat16),
        compiler_params=pltpu.CompilerParams(vmem_limit_bytes=12 * MIB),
        cost_estimate=pl.CostEstimate(flops=0, bytes_accessed=8 * groups * width * depth, transcendentals=0),
        name="turn",
    )(*arrays)


def closed_walk(i, members):
    return jnp.where(i < members // 2, i, members - 1 - i + members // 2)


def stack_kernel(scale, left_first, first_group, layout, left_ref, *refs):
    out_ref = refs[-1]
    pair, _, width, _ = left_ref.shape[1:]
    step_groups = out_ref.shape[0] // pair
    members = len(layout)
    where = closed_walk(lax.axis_index("chan"), members)
    for s in range(step_groups):
        g = pl.program_id(0) * step_groups + s
        for step, items in layout:
            right = jnp.concatenate(sum([gathered(refs[i], first_group + g, place) for i, place in items], []), 0)
            column = closed_walk(lax.rem(where + (step + members), members), members)
            columns = pl.ds(pl.multiple_of(column * width, width), width)
            left = left_ref[first_group - left_first + g].reshape(pair * 2 * width, -1)
            product = jnp.dot(left, right, preferred_element_type=jnp.float32) * scale
            out_ref[s * pair : (s + 1) * pair, :, :, columns] = product.astype(jnp.bfloat16).reshape(pair, 2, width, width)


def stack(left, left_first, steps, into, first_group, groups, bins, sources):
    members = len(steps)
    _, pair, _, width, depth = left.shape
    step_groups = max(n for n in range(1, STEP_GROUPS + 1) if groups % n == 0 and first_group % n == 0)
    arrays, places = operands_of(sum([views for _, views in steps], []))
    layout = []
    for step, views in steps:
        layout.append((step, places[: len(views)]))
        places = places[len(views) :]
    operands = [left, *arrays]
    in_specs = in_vmem(len(operands))
    aliases = {}
    if into is not None:
        aliases = {len(operands): 0}
        operands.append(into)
        in_specs.append(pl.BlockSpec(memory_space=pl.ANY))
    block = (step_groups * pair, 2, width, members * width)
    return pl.pallas_call(
        functools.partial(stack_kernel, 1.0 / math.sqrt(sources), left_first, first_group, layout),
        grid=(groups // step_groups,),
        in_specs=in_specs,
        out_specs=pl.BlockSpec(block, lambda g: (first_group // step_groups + g, 0, 0, 0)),
        out_shape=jax.ShapeDtypeStruct((bins, 2, width, members * width), jnp.bfloat16),
        input_output_aliases=aliases,
        compiler_params=pltpu.CompilerParams(vmem_limit_bytes=24 * MIB, dimension_semantics=("arbitrary",)),
        cost_estimate=pl.CostEstimate(
            flops=4 * groups * pair * depth * width * width * members,
            bytes_accessed=4 * groups * pair * width * members * width,
            transcendentals=0,
        ),
        name="stack",
    )(*operands)


def after(arrays, *earlier):
    return list(lax.optimization_barrier((tuple(arrays), earlier))[0])


def ring_walk(members):
    ring = [i if i < members // 2 else members - 1 - i + members // 2 for i in range(members)]
    return [(ring[i], ring[(i + 1) % members]) for i in range(members)]


def halves_of(views, total):
    first, second, seen = [], [], 0
    for view in views:
        cut_at = min(max(total // 2 - seen, 0), view[2])
        first += [part_of(view, 0, cut_at)] if cut_at else []
        second += [part_of(view, cut_at, view[2])] if cut_at < view[2] else []
        seen += view[2]
    return first, second


def ring_phase(travellers, members):
    ahead = ring_walk(members)
    moved = []
    for way, pairs in ((0, ahead), (1, [(b, a) for a, b in ahead])):
        sent, places = join(sum([views[way] for views in travellers], []))
        came = lax.ppermute(sent, "chan", pairs)
        moved.append([(came, *place) for place in places])
    result = []
    for views in travellers:
        result.append((moved[0][: len(views[0])], moved[1][: len(views[1])]))
        moved = [moved[0][len(views[0]) :], moved[1][len(views[1]) :]]
    return result


def chunk_starts(share):
    total, starts, seen = sum(CHUNK_WEIGHTS), [0], 0
    for weight in CHUNK_WEIGHTS:
        seen += weight
        starts.append(round(share * seen / total))
    return starts


def local(dests, members, raw, offsets, quality):
    windows = raw.shape[0]
    pair = 16 // (2 * windows)
    bins = F // dests
    share = bins // pair
    chips = dests // 2
    assert chips & (chips - 1) == 0
    starts = chunk_starts(share)
    chunks = list(zip(starts[:-1], starts[1:]))
    table = jnp.asarray(dft_table())

    keep, give = spectra(raw, offsets, quality, table, dests)
    other = lax.ppermute(give, "win", [(i, i ^ 1) for i in range(dests)])
    def travel(n, *earlier):
        start, stop = chunks[n]
        came = []
        for k in range(1, chips):
            sent, _ = join([(x, k * share + start, 1, stop - start, start) for x in (keep, other)])
            if earlier:
                sent = after([sent], *earlier)[0]
            came.append(lax.ppermute(sent, "win", [(i, i ^ (2 * k)) for i in range(dests)]))
        return [(x, 0, 2, stop - start, start) for x in came]

    units = [[(x, 0, 1, share, 0) for x in (keep, other)]]
    turns = members // 2
    found = [[(0, units[0])]]
    lefts = []
    held = [(units[0], units[0])]
    out = None
    stacked = 0
    for phase in range(len(chunks) + turns):
        travellers, who = [], []
        for u in range(len(units)):
            step = phase - u + 1
            if not 1 <= step <= turns:
                continue
            left, right = held[u]
            if step == turns:
                total = sum(view[2] for view in left)
                left, right = halves_of(left, total)[0], halves_of(right, total)[1]
            travellers.append((left, right))
            who.append((u, step))
        if 0 < phase - turns + 1 <= len(chunks):
            start, stop = chunks[phase - turns]
            lefts.append(turn(found[0][0][1] + found[phase - turns + 1][0][1], start, stop - start, windows))
            left, right = travellers[0]
            tied = after([left[0][0]], lefts[-1])[0]
            travellers[0] = ([(tied, *left[0][1:])] + left[1:], right)
        if phase < len(chunks):
            arrives = travel(phase, *([x[0] for x in units[-1][:1]] if phase else []))
        for (u, step), (left, right) in zip(who, ring_phase(travellers, members)):
            held[u] = (left, right)
            if step == turns:
                found[u].append((turns, left + right))
            else:
                found[u] += [(-step, left), (step, right)]
        if phase < len(chunks):
            units.append(arrives)
            held.append((arrives, arrives))
            found.append([(0, arrives)])
        while stacked < phase - turns or (phase + 1 == len(chunks) + turns and stacked < len(chunks)):
            start, stop = chunks[stacked]
            steps = [(a[0], a[1] + b[1]) for a, b in zip(found[0], found[stacked + 1])]
            out = stack(lefts[stacked], start, steps, out, start, stop - start, bins, dests * windows)
            stacked += 1
    return out


def solution(mesh):
    in_specs = (P("win", None, "chan"), P("win"), P("win", "chan"))
    out_specs = P("win", None, "chan", None)
    run = functools.partial(local, mesh.shape["win"], mesh.shape["chan"])
    return jax.shard_map(run, mesh=mesh, in_specs=in_specs, out_specs=out_specs, check_vma=False)
```

```python
import functools
import math

import jax
import jax.numpy as jnp
import ml_dtypes
import numpy as np
from jax import lax
from jax.experimental import pallas as pl
from jax.experimental.pallas import tpu as pltpu
from jax.sharding import PartitionSpec as P

F = 384
L = 3072
FIRST_BIN = 60
CHUNK_WEIGHTS = (10, 8, 6)
STEP_GROUPS = 2
SPECTRA_MIB = 50

epsilon = 1e-05
MIB = 1024 * 1024


def dft_table():
    sample_idx = np.arange(L, dtype=np.int64)
    bin_idx = FIRST_BIN + np.arange(F, dtype=np.int64)
    residue = bin_idx[:, None] * sample_idx[None, :] % L
    angles = residue.astype(np.float32) * np.float32(2.0 * math.pi / L)
    return np.concatenate([np.cos(angles), -np.sin(angles)], 0).astype(ml_dtypes.bfloat16)


def interleave(windows, bins):
    pair = 16 // (2 * windows)
    rows = 2 * windows * bins
    row = lax.broadcasted_iota(jnp.int32, (rows, rows), 0)
    col = lax.broadcasted_iota(jnp.int32, (rows, rows), 1)
    w, p = row & (windows - 1), (row >> 3) & 1
    b, g = (row & 7) >> (windows.bit_length() - 1), row >> 4
    return jnp.where(col == (w * 2 + p) * bins + g * pair + b, 1.0, 0.0).astype(jnp.bfloat16)


def cut(raw_ref, slot, shift_at, window_ref):
    width = raw_ref.shape[2]
    spare = raw_ref.shape[1] - L
    tile = 256
    base = jnp.minimum(shift_at // 16, (spare - 16) // 16) * 16
    rest = shift_at - base
    whole = rest // 8
    fine = rest - whole * 8
    back = jnp.where(fine == 0, 0, 8 - fine)
    keep = lax.broadcasted_iota(jnp.int32, (tile // 8, 8, width), 1) < 8 - fine
    count = tile // 8
    for step in range(L // tile):
        start = pl.multiple_of(base + step * tile, 16)
        rows = raw_ref[slot, pl.ds(start, tile + 16), :].astype(jnp.float32).reshape(count + 2, 8, width)
        rolled = pltpu.roll(rows, back, 1)
        upper = jnp.where(whole == 0, rolled[1 : count + 1], rolled[2:])
        lower = jnp.where(whole == 0, rolled[:count], jnp.where(whole == 1, rolled[1 : count + 1], rolled[2:]))
        moved = jnp.where(keep, lower, upper)
        window_ref[step * tile : (step + 1) * tile, :] = moved.reshape(tile, width).astype(jnp.bfloat16)


def spectra_kernel(chips, offsets_ref, table_hbm, raw_hbm, quality_hbm, keep_ref, give_ref, *scratch):
    table_ref, quality_ref, raw_ref, white, mixed, sems = scratch[:6]
    cuts = scratch[6:]
    windows, _, width = raw_ref.shape
    loads = [pltpu.make_async_copy(raw_hbm.at[w], raw_ref.at[w], sems.at[w]) for w in range(windows)]
    table_load = pltpu.make_async_copy(table_hbm, table_ref, sems.at[windows])
    quality_load = pltpu.make_async_copy(quality_hbm, quality_ref, sems.at[windows + 1])
    early = min(2, windows)
    for load in (*loads[:early], table_load, *loads[early:], quality_load):
        load.start()
    mix = interleave(windows, 256 // (2 * windows))
    for w in range(early):
        loads[w].wait()
        cut(raw_ref, w, offsets_ref[w], cuts[w])
    for load in (table_load, *loads[early:], quality_load):
        load.wait()
    for w in range(windows):
        if w + early < windows:
            cut(raw_ref, w + early, offsets_ref[w + early], cuts[w + early])
        transform = jnp.dot(table_ref[...], cuts[w][...], preferred_element_type=jnp.float32)
        band_power = jnp.sum(transform * transform, axis=0, keepdims=True) / F
        usable = quality_ref[w : w + 1, :].astype(jnp.float32)
        white[w] = (transform * (lax.rsqrt(band_power + epsilon) * usable)).astype(jnp.bfloat16)

    pair = 16 // (2 * windows)
    bins = mix.shape[0] // (2 * windows)
    groups = bins // pair
    for block in range(F // bins):
        parts = [
            white[v, p * F + block * bins : p * F + (block + 1) * bins, :] for v in range(windows) for p in range(2)
        ]
        product = jnp.dot(mix, jnp.concatenate(parts, 0), preferred_element_type=jnp.float32)
        mixed[block * groups : (block + 1) * groups] = product.astype(jnp.bfloat16).reshape(groups, 16, width)
    me = lax.axis_index("win")
    chip, core = me // 2, me % 2
    share = keep_ref.shape[0] // chips
    for k in range(chips):
        at = (chip ^ k) * 2 * share
        keep_ref[k * share : (k + 1) * share] = mixed[pl.ds(at + core * share, share)]
        give_ref[k * share : (k + 1) * share] = mixed[pl.ds(at + (1 - core) * share, share)]


def in_vmem(count):
    return [pl.BlockSpec(memory_space=pltpu.VMEM)] * count


def spectra(raw, offsets, quality, table, dests):
    windows, _, width = raw.shape
    groups = F * 2 * windows // 16
    blocks = (groups // 2, 16, width)
    return pl.pallas_call(
        functools.partial(spectra_kernel, dests // 2),
        in_specs=[pl.BlockSpec(memory_space=pltpu.SMEM)] + [pl.BlockSpec(memory_space=pl.ANY)] * 3,
        out_specs=in_vmem(2),
        scratch_shapes=[
            pltpu.VMEM(table.shape, table.dtype),
            pltpu.VMEM(quality.shape, quality.dtype),
            pltpu.VMEM(raw.shape, raw.dtype),
            pltpu.VMEM((windows, 2 * F, width), jnp.bfloat16),
            pltpu.VMEM((groups, 16, width), jnp.bfloat16),
            pltpu.SemaphoreType.DMA((windows + 2,)),
            *[pltpu.VMEM((L, width), jnp.bfloat16)] * windows,
        ],
        out_shape=[jax.ShapeDtypeStruct(blocks, jnp.bfloat16)] * 2,
        compiler_params=pltpu.CompilerParams(vmem_limit_bytes=SPECTRA_MIB * MIB),
        cost_estimate=pl.CostEstimate(
            flops=2 * windows * 2 * F * L * width, bytes_accessed=2 * windows * raw.shape[1] * width + 4 * F * L, transcendentals=0
        ),
        name="spectra",
    )(offsets, table, raw, quality)


def part_of(view, low, high):
    x, base, _, groups, first = view
    return (x, base + low * groups, high - low, groups, first)


def join_kernel(moves, *refs):
    out_ref = refs[-1]
    to = 0
    for i, at, count in moves:
        out_ref[to : to + count] = refs[i][at : at + count]
        to += count


def join(views):
    arrays, moves, places, to = [], [], [], 0
    for x, base, sources, groups, first in views:
        known = [i for i, y in enumerate(arrays) if y is x]
        if not known:
            arrays.append(x)
        moves.append((known[0] if known else len(arrays) - 1, base, sources * groups))
        places.append((to, sources, groups, first))
        to += sources * groups
    shape = (to, *arrays[0].shape[1:])
    joined = pl.pallas_call(
        functools.partial(join_kernel, moves),
        in_specs=in_vmem(len(arrays)),
        out_specs=in_vmem(1)[0],
        out_shape=jax.ShapeDtypeStruct(shape, arrays[0].dtype),
        compiler_params=pltpu.CompilerParams(vmem_limit_bytes=12 * MIB),
        cost_estimate=pl.CostEstimate(flops=0, bytes_accessed=4 * math.prod(shape), transcendentals=0),
        name="join",
    )(*arrays)
    return joined, places


def gathered(ref, group, place):
    base, sources, groups, first = place
    return [ref[base + source * groups + group - first] for source in range(sources)]


def operands_of(views):
    arrays, places = [], []
    for x, *place in views:
        known = [i for i, y in enumerate(arrays) if y is x]
        if not known:
            arrays.append(x)
        places.append((known[0] if known else len(arrays) - 1, place))
    return arrays, places


def turn_kernel(windows, first_group, views, *refs):
    out_ref = refs[-1]
    _, pair, _, width, depth = out_ref.shape
    bin_of = lax.broadcasted_iota(jnp.int32, (width, depth), 1) % 8 // windows

    def body(g, carry):
        x = jnp.concatenate(sum([gathered(refs[i], first_group + g, place) for i, place in views], []), 0)
        by_part = x.astype(jnp.float32).reshape(depth // 16, 16, width)
        turned = jnp.concatenate([by_part[:, 8:], -by_part[:, :8]], 1)
        for part, rows in enumerate((by_part, turned)):
            left = rows.reshape(depth, width).T
            for b in range(pair):
                out_ref[g, b, part] = jnp.where(bin_of == b, left, 0.0).astype(jnp.bfloat16)
        return carry

    lax.fori_loop(0, out_ref.shape[0], body, 0)


def turn(views, first_group, groups, windows):
    arrays, places = operands_of(views)
    rows, width = arrays[0].shape[1:]
    depth = sum(place[1] for _, place in places) * rows
    pair = 16 // (2 * windows)
    return pl.pallas_call(
        functools.partial(turn_kernel, windows, first_group, places),
        in_specs=in_vmem(len(arrays)),
        out_specs=in_vmem(1)[0],
        out_shape=jax.ShapeDtypeStruct((groups, pair, 2, width, depth), jnp.bfloat16),
        compiler_params=pltpu.CompilerParams(vmem_limit_bytes=12 * MIB),
        cost_estimate=pl.CostEstimate(flops=0, bytes_accessed=8 * groups * width * depth, transcendentals=0),
        name="turn",
    )(*arrays)


def closed_walk(i, members):
    return jnp.where(i < members // 2, i, members - 1 - i + members // 2)


def stack_kernel(scale, left_first, first_group, layout, left_ref, *refs):
    out_ref = refs[-1]
    pair, _, width, _ = left_ref.shape[1:]
    step_groups = out_ref.shape[0] // pair
    members = len(layout)
    where = closed_walk(lax.axis_index("chan"), members)
    for s in range(step_groups):
        g = pl.program_id(0) * step_groups + s
        for step, items in layout:
            right = jnp.concatenate(sum([gathered(refs[i], first_group + g, place) for i, place in items], []), 0)
            column = closed_walk(lax.rem(where + (step + members), members), members)
            columns = pl.ds(pl.multiple_of(column * width, width), width)
            for b in range(pair):
                for part in range(2):
                    left = left_ref[first_group - left_first + g, b, part]
                    product = jnp.dot(left, right, preferred_element_type=jnp.float32)
                    out_ref[s * pair + b, part, :, columns] = (product * scale).astype(jnp.bfloat16)


def stack(left, left_first, steps, into, first_group, groups, bins, sources):
    members = len(steps)
    _, pair, _, width, depth = left.shape
    step_groups = max(n for n in range(1, STEP_GROUPS + 1) if groups % n == 0 and first_group % n == 0)
    arrays, places = operands_of(sum([views for _, views in steps], []))
    layout = []
    for step, views in steps:
        layout.append((step, places[: len(views)]))
        places = places[len(views) :]
    operands = [left, *arrays]
    in_specs = in_vmem(len(operands))
    aliases = {}
    if into is not None:
        aliases = {len(operands): 0}
        operands.append(into)
        in_specs.append(pl.BlockSpec(memory_space=pl.ANY))
    block = (step_groups * pair, 2, width, members * width)
    return pl.pallas_call(
        functools.partial(stack_kernel, 1.0 / math.sqrt(sources), left_first, first_group, layout),
        grid=(groups // step_groups,),
        in_specs=in_specs,
        out_specs=pl.BlockSpec(block, lambda g: (first_group // step_groups + g, 0, 0, 0)),
        out_shape=jax.ShapeDtypeStruct((bins, 2, width, members * width), jnp.bfloat16),
        input_output_aliases=aliases,
        compiler_params=pltpu.CompilerParams(vmem_limit_bytes=24 * MIB, dimension_semantics=("arbitrary",)),
        cost_estimate=pl.CostEstimate(
            flops=4 * groups * pair * depth * width * width * members,
            bytes_accessed=4 * groups * pair * width * members * width,
            transcendentals=0,
        ),
        name="stack",
    )(*operands)


def after(arrays, *earlier):
    return list(lax.optimization_barrier((tuple(arrays), earlier))[0])


def ring_walk(members):
    ring = [i if i < members // 2 else members - 1 - i + members // 2 for i in range(members)]
    return [(ring[i], ring[(i + 1) % members]) for i in range(members)]


def halves_of(views, total):
    first, second, seen = [], [], 0
    for view in views:
        cut_at = min(max(total // 2 - seen, 0), view[2])
        first += [part_of(view, 0, cut_at)] if cut_at else []
        second += [part_of(view, cut_at, view[2])] if cut_at < view[2] else []
        seen += view[2]
    return first, second


def ring_phase(travellers, members):
    ahead = ring_walk(members)
    moved = []
    for way, pairs in ((0, ahead), (1, [(b, a) for a, b in ahead])):
        sent, places = join(sum([views[way] for views in travellers], []))
        came = lax.ppermute(sent, "chan", pairs)
        moved.append([(came, *place) for place in places])
    result = []
    for views in travellers:
        result.append((moved[0][: len(views[0])], moved[1][: len(views[1])]))
        moved = [moved[0][len(views[0]) :], moved[1][len(views[1]) :]]
    return result


def chunk_starts(share):
    total, starts, seen = sum(CHUNK_WEIGHTS), [0], 0
    for weight in CHUNK_WEIGHTS:
        seen += weight
        starts.append(round(share * seen / total))
    return starts


def local(dests, members, raw, offsets, quality):
    windows = raw.shape[0]
    pair = 16 // (2 * windows)
    bins = F // dests
    share = bins // pair
    chips = dests // 2
    assert chips & (chips - 1) == 0
    starts = chunk_starts(share)
    chunks = list(zip(starts[:-1], starts[1:]))
    table = jnp.asarray(dft_table())

    keep, give = spectra(raw, offsets, quality, table, dests)
    other = lax.ppermute(give, "win", [(i, i ^ 1) for i in range(dests)])
    def travel(n, *earlier):
        start, stop = chunks[n]
        came = []
        for k in range(1, chips):
            sent, _ = join([(x, k * share + start, 1, stop - start, start) for x in (keep, other)])
            if earlier:
                sent = after([sent], *earlier)[0]
            came.append(lax.ppermute(sent, "win", [(i, i ^ (2 * k)) for i in range(dests)]))
        return [(x, 0, 2, stop - start, start) for x in came]

    units = [[(x, 0, 1, share, 0) for x in (keep, other)]]
    turns = members // 2
    found = [[(0, units[0])]]
    lefts = []
    held = [(units[0], units[0])]
    out = None
    stacked = 0
    for phase in range(len(chunks) + turns):
        travellers, who = [], []
        for u in range(len(units)):
            step = phase - u + 1
            if not 1 <= step <= turns:
                continue
            left, right = held[u]
            if step == turns:
                total = sum(view[2] for view in left)
                left, right = halves_of(left, total)[0], halves_of(right, total)[1]
            travellers.append((left, right))
            who.append((u, step))
        if 0 < phase - turns + 1 <= len(chunks):
            start, stop = chunks[phase - turns]
            lefts.append(turn(found[0][0][1] + found[phase - turns + 1][0][1], start, stop - start, windows))
            left, right = travellers[0]
            tied = after([left[0][0]], lefts[-1])[0]
            travellers[0] = ([(tied, *left[0][1:])] + left[1:], right)
        if phase < len(chunks):
            arrives = travel(phase, *([x[0] for x in units[-1][:1]] if phase else []))
        for (u, step), (left, right) in zip(who, ring_phase(travellers, members)):
            held[u] = (left, right)
            if step == turns:
                found[u].append((turns, left + right))
            else:
                found[u] += [(-step, left), (step, right)]
        if phase < len(chunks):
            units.append(arrives)
            held.append((arrives, arrives))
            found.append([(0, arrives)])
        while stacked < phase - turns or (phase + 1 == len(chunks) + turns and stacked < len(chunks)):
            start, stop = chunks[stacked]
            steps = [(a[0], a[1] + b[1]) for a, b in zip(found[0], found[stacked + 1])]
            out = stack(lefts[stacked], start, steps, out, start, stop - start, bins, dests * windows)
            stacked += 1
    return out


def solution(mesh):
    in_specs = (P("win", None, "chan"), P("win"), P("win", "chan"))
    out_specs = P("win", None, "chan", None)
    run = functools.partial(local, mesh.shape["win"], mesh.shape["chan"])
    return jax.shard_map(run, mesh=mesh, in_specs=in_specs, out_specs=out_specs, check_vma=False)
```
